32 devices in a mesh: group: 2 (over y), adapter: 4 (over x, core), tensor: 4 (over z).
Axes of the slice: x: 2, y: 2, z: 4, core: 2. Of those that a mesh axis runs over, the one named last changes fastest.
Arguments:
- queries: bfloat16 [512, 2, 8192], P(('group', 'adapter'), None, 'tensor'), parts along dimension 0, may hold values from -240 to 240
- token_key_rows: bfloat16 [512, 2, 1024], P(('group', 'adapter'), None, 'tensor'), parts along dimension 0, may hold values from -4 to 4
- token_value_rows: bfloat16 [512, 2, 1024], P(('group', 'adapter'), None, 'tensor'), parts along dimension 0, may hold values from -4 to 4
- cached_key_rows: bfloat16 [512, 128, 1024], P(('group', 'adapter'), None, 'tensor'), parts along dimension 0, may hold values from -4 to 4
- cached_value_rows: bfloat16 [512, 128, 1024], P(('group', 'adapter'), None, 'tensor'), parts along dimension 0, may hold values from -4 to 4
- cache_length: int32 [512], P(('group', 'adapter')), parts along dimension 0, may hold values from 16 to 128
- request_adapter: int32 [512], P(('group', 'adapter')), parts along dimension 0, may hold values from 0 to 15, as said below
- output_weight_matrix: bfloat16 [8192, 4096], P('tensor'), may hold values from -0.0625 to 0.0625
- adapter_down_weight: bfloat16 [32, 64, 8192], P(('group', 'adapter'), None, 'tensor'), parts along dimension 0, may hold values from -0.0625 to 0.0625
- adapter_up_weight: bfloat16 [32, 64, 4096], P(('group', 'adapter'), None, 'tensor'), parts along dimension 0, may hold values from -0.75 to 0.75
Outputs:
- mixed: bfloat16 [512, 2, 4096], P(('group', 'adapter'), None, 'tensor'), parts along dimension 0
The draws below stay inside these ranges and needn't reach their ends.
There are 2 independent parts, one for each index of `group`. The reference program is written for one: setup_inputs(seed, part) draws one part's arguments, and reference() takes and returns one part's arrays. A program takes and returns all parts, laid end to end along the dimension named above; an argument that names none is the same for every part. Nothing has to cross between parts.
Inputs may be any that keep to these rules, and one draw needn't show every extreme that they name: `request_adapter`: adapter a is resident on owner a // 4. In every aligned block of 64 requests at most 32 requests name adapters of one owner.
All inputs are finite; a program needn't handle non-finite values.
Results may differ from the reference program's by a relative error of at most 0.014.
Values may be sent and summed in bfloat16 or wider, within the bound.
No kernel may reach another device: no remote copies, remote signals or barrier semaphores. Data moves between devices by JAX's collectives and lax.ppermute only.
A program may use at most 128 MiB of HBM per device.

```python
import math
import jax
import jax.numpy as jnp
from jax import lax

HEADS = 64
KV_HEADS = 8
HEAD_DIM = 128
OUTPUT_FEATURES = 4096
ADAPTER_RANK = 64
STEPS = 2
ROWS_DEV = 64
MAXLEN = 128
ADP_DEV = 4
CAP = 32
FEATURE_DIM = 8192
ROWS = 256
ADAPTER_TOTAL = 16
N_TENSOR = 4


def base_keys(key):
    noise = jax.random.normal(jax.random.fold_in(key, 5), (ROWS, MAXLEN, KV_HEADS * HEAD_DIM), jnp.float32)
    return jnp.clip(noise, -4.0, 4.0)


def draw_cached_key_rows(key, part):
    cached = base_keys(key)
    return cached.astype(jnp.bfloat16)


def draw_queries(key, part):
    key = jax.random.fold_in(key, 14)
    values = jnp.clip(jax.random.normal(key, (ROWS, STEPS, HEADS * HEAD_DIM), jnp.float32), -4.0, 4.0)
    return values.astype(jnp.bfloat16)


def draw_cache_length(key, part):
    key = jax.random.fold_in(key, 12)
    lengths = jax.random.randint(jax.random.fold_in(key, 1), (ROWS,), MAXLEN // 8, MAXLEN + 1, jnp.int32)
    chosen = jax.random.randint(jax.random.fold_in(key, 2), (), 0, ROWS, jnp.int32)
    return jnp.where(jnp.arange(ROWS, dtype=jnp.int32) == chosen, MAXLEN, lengths).astype(jnp.int32)


def draw_request_adapter(key, part):
    key = jax.random.fold_in(key, 11)
    owner_count = ADAPTER_TOTAL // ADP_DEV
    hottest = jax.random.randint(jax.random.fold_in(key, 1), (), 0, owner_count, jnp.int32)
    spare = ROWS_DEV - CAP
    candidates = (hottest + 1 + jnp.arange((owner_count - 1) * CAP, dtype=jnp.int32) // CAP) % owner_count

    def one_block(block_key):
        taken = jax.random.permutation(jax.random.fold_in(block_key, 1), candidates)[:spare]
        owners_here = jnp.concatenate([jnp.full((CAP,), hottest, jnp.int32), taken])
        return jax.random.permutation(jax.random.fold_in(block_key, 2), owners_here)
    block_keys = jax.random.split(jax.random.fold_in(key, 2), owner_count)
    owners_all = jax.vmap(one_block)(block_keys).reshape(ROWS)
    resident_adapters = jax.random.randint(jax.random.fold_in(key, 3), (ROWS,), 0, ADP_DEV, jnp.int32)
    return (owners_all * ADP_DEV + resident_adapters).astype(jnp.int32)


def block_levels(rng, shape, cuts, low, top_value):
    def one(dim, parts):
        steps = jax.random.uniform(jax.random.fold_in(jax.random.fold_in(rng, 6), dim), (parts,), jnp.float32, low / len(cuts), top_value / len(cuts))
        return jnp.repeat(jnp.exp(steps), shape[dim] // parts).reshape((-1,) + (1,) * (len(shape) - dim - 1))

    factor_of = one(*cuts[0])
    for cut in cuts[1:]:
        factor_of = factor_of * one(*cut)
    return factor_of


def centred(own_key, extent, width, reach, cuts=(), held_as=jnp.bfloat16):
    drawn = width * jax.random.normal(own_key, extent, jnp.float32)
    if cuts:
        drawn = drawn * block_levels(own_key, extent, cuts, -0.22, 0.18)
    return jnp.clip(drawn, -reach, reach).astype(held_as)


def setup_inputs(seed: int = 0, part: int = 0) -> dict:
    splits = jax.random.split(jax.random.key(seed), 11)
    part_splits = jax.random.split(jax.random.fold_in(splits[10], part), 11)
    queries = draw_queries(jax.random.fold_in(jax.random.fold_in(splits[10], part), 71), part)
    token_key_rows = centred(part_splits[1], (ROWS, STEPS, KV_HEADS * HEAD_DIM), 1.0, 4.0, ((0, 4), (2, 4)))
    token_value_rows = centred(part_splits[2], (ROWS, STEPS, KV_HEADS * HEAD_DIM), 1.0, 4.0, ((0, 4), (2, 4)))
    cached_key_rows = draw_cached_key_rows(jax.random.fold_in(jax.random.fold_in(splits[10], part), 71), part)
    cached_value_rows = centred(part_splits[4], (ROWS, MAXLEN, KV_HEADS * HEAD_DIM), 1.0, 4.0, ((0, 4), (2, 4)))
    cache_length = draw_cache_length(jax.random.fold_in(jax.random.fold_in(splits[10], part), 71), part)
    request_adapter = draw_request_adapter(jax.random.fold_in(jax.random.fold_in(splits[10], part), 71), part)
    output_weight_matrix = centred(splits[7], (FEATURE_DIM, OUTPUT_FEATURES), FEATURE_DIM ** -0.5, 0.0625, ((0, 4),))
    adapter_down_weight = centred(part_splits[8], (ADAPTER_TOTAL, ADAPTER_RANK, FEATURE_DIM), FEATURE_DIM ** -0.5, 0.0625, ((0, 4), (2, 4)))
    adapter_up_weight = centred(part_splits[9], (ADAPTER_TOTAL, ADAPTER_RANK, OUTPUT_FEATURES), ADAPTER_RANK ** -0.5, 0.75, ((0, 4), (2, 4)))
    return dict(queries=queries, token_key_rows=token_key_rows, token_value_rows=token_value_rows, cached_key_rows=cached_key_rows, cached_value_rows=cached_value_rows, cache_length=cache_length, request_adapter=request_adapter, output_weight_matrix=output_weight_matrix, adapter_down_weight=adapter_down_weight, adapter_up_weight=adapter_up_weight)


NEGATIVE = -1e+30

def attend(queries, token_key_rows, token_value_rows, cached_key_rows, cached_value_rows, cache_length):
    row_count = queries.shape[0]
    groups = cached_key_rows.shape[2] // HEAD_DIM
    sharing = queries.shape[2] // HEAD_DIM // groups
    scaling = 1.0 / math.sqrt(HEAD_DIM)
    query_f = queries.astype(jnp.float32).reshape(row_count, STEPS, groups, sharing, HEAD_DIM)
    cache_k = cached_key_rows.astype(jnp.float32).reshape(row_count, MAXLEN, groups, HEAD_DIM)
    cache_v = cached_value_rows.astype(jnp.float32).reshape(row_count, MAXLEN, groups, HEAD_DIM)
    fresh_k = token_key_rows.astype(jnp.float32).reshape(row_count, STEPS, groups, HEAD_DIM)
    fresh_v = token_value_rows.astype(jnp.float32).reshape(row_count, STEPS, groups, HEAD_DIM)
    cache_scores = jnp.einsum('rsgqd,rlgd->rsgql', query_f, cache_k) * scaling
    fresh_scores = jnp.einsum('rsgqd,rtgd->rsgqt', query_f, fresh_k) * scaling
    positions = jnp.arange(MAXLEN, dtype=jnp.int32)
    live_cache = (positions[None, :] < cache_length[:, None])[:, None, None, None, :]
    tokens = jnp.arange(STEPS, dtype=jnp.int32)
    live_fresh = (tokens[None, :] <= tokens[:, None])[None, :, None, None, :]
    cache_scores = jnp.where(live_cache, cache_scores, NEGATIVE)
    fresh_scores = jnp.where(live_fresh, fresh_scores, NEGATIVE)
    highest = jnp.maximum(lax.optimization_barrier(jnp.max(cache_scores, axis=-1)), lax.optimization_barrier(jnp.max(fresh_scores, axis=-1)))
    cache_weight = jnp.exp(cache_scores - highest[..., None])
    fresh_weight = jnp.exp(fresh_scores - highest[..., None])
    denominator = lax.optimization_barrier(jnp.sum(cache_weight, axis=-1)) + lax.optimization_barrier(jnp.sum(fresh_weight, axis=-1))
    cache_round = lax.optimization_barrier(cache_weight.astype(jnp.bfloat16)).astype(jnp.float32)
    fresh_round = lax.optimization_barrier(fresh_weight.astype(jnp.bfloat16)).astype(jnp.float32)
    numerator = jnp.einsum('rsgql,rlgd->rsgqd', cache_round, cache_v)
    numerator = numerator + jnp.einsum('rsgqt,rtgd->rsgqd', fresh_round, fresh_v)
    attended = (numerator / denominator[..., None]).astype(jnp.bfloat16)
    return attended.reshape(row_count, STEPS, groups * sharing * HEAD_DIM)

def reference(queries, token_key_rows, token_value_rows, cached_key_rows, cached_value_rows, cache_length, request_adapter, output_weight_matrix, adapter_down_weight, adapter_up_weight):
    attended = attend(queries, token_key_rows, token_value_rows, cached_key_rows, cached_value_rows, cache_length)
    flattened_rows = attended.reshape(ROWS * STEPS, FEATURE_DIM)
    block_width = FEATURE_DIM // N_TENSOR
    base = jnp.zeros((ROWS * STEPS, OUTPUT_FEATURES), jnp.float32)
    for block in range(N_TENSOR):
        piece = jnp.dot(flattened_rows[:, block * block_width:(block + 1) * block_width], output_weight_matrix[block * block_width:(block + 1) * block_width], preferred_element_type=jnp.float32).astype(jnp.bfloat16)
        base = base + lax.optimization_barrier(piece).astype(jnp.float32)
    request_ids = jnp.repeat(request_adapter, STEPS)
    all_low_projected = lax.dot_general(flattened_rows, adapter_down_weight.reshape(ADAPTER_TOTAL * ADAPTER_RANK, FEATURE_DIM), (((1,), (1,)), ((), ())), preferred_element_type=jnp.float32)
    picked = request_ids[:, None] == jnp.arange(ADAPTER_TOTAL, dtype=jnp.int32)[None, :]
    low_rank = lax.optimization_barrier(jnp.sum(all_low_projected.reshape(ROWS * STEPS, ADAPTER_TOTAL, ADAPTER_RANK) * picked[..., None].astype(jnp.float32), axis=1))
    low_rank = low_rank.astype(jnp.bfloat16)
    spread_rows = (low_rank[:, None, :] * picked[..., None].astype(jnp.bfloat16)).reshape(ROWS * STEPS, ADAPTER_TOTAL * ADAPTER_RANK)
    low_rank_update = jnp.dot(spread_rows, adapter_up_weight.reshape(ADAPTER_TOTAL * ADAPTER_RANK, OUTPUT_FEATURES), preferred_element_type=jnp.float32)
    return (base + low_rank_update).astype(jnp.bfloat16).reshape(ROWS, STEPS, OUTPUT_FEATURES)
```

```python
import functools
import math

import jax
import jax.numpy as jnp
from jax import lax
from jax.experimental import pallas as pl
from jax.experimental.pallas import tpu as pltpu
from jax.sharding import PartitionSpec as P

HEAD_DIM = 128
NEGATIVE = -1e30
LANES = 128
VMEM_LIMIT = 56 * 1024 * 1024

F32 = jnp.float32
BF16 = jnp.bfloat16


def contract(a, b, a_dim, b_dim):
    return lax.dot_general(
        a, b, (((a_dim,), (b_dim,)), ((), ())), preferred_element_type=F32
    )


def attend_kernel(
    owners,
    resident,
    capacity,
    lengths,
    place,
    adapters,
    queries,
    fresh_k,
    fresh_v,
    cache_k,
    cache_v,
    attended,
    placing_out,
    *rest,
):
    packed = rest[:owners]
    query_scratch, result_scratch = rest[owners:]
    step = pl.program_id(0)
    block, steps, width = queries.shape
    heads = width // HEAD_DIM
    groups = cache_k.shape[2] // HEAD_DIM
    sharing = heads // groups
    cache_size = cache_k.shape[1]
    rows = block * steps
    total_rows = attended.shape[0]
    span = steps * sharing
    scaling = 1.0 / math.sqrt(HEAD_DIM)

    flat = queries[...].astype(F32).reshape(rows, width)
    for h in range(heads):
        query_scratch[h * rows : (h + 1) * rows, :] = flat[:, h * HEAD_DIM : (h + 1) * HEAD_DIM]
    new_k = fresh_k[...].reshape(rows, groups * HEAD_DIM)
    new_v = fresh_v[...].reshape(rows, groups * HEAD_DIM)

    positions = lax.broadcasted_iota(jnp.int32, (span, cache_size), 1)
    row_id = lax.broadcasted_iota(jnp.int32, (block * span, rows), 0)
    col_id = lax.broadcasted_iota(jnp.int32, (block * span, rows), 1)
    same = lax.div(row_id, span) == lax.div(col_id, steps)
    causal = lax.rem(col_id, steps) <= lax.div(lax.rem(row_id, span), sharing)
    live_fresh = jnp.logical_and(same, causal)

    for g in range(groups):
        lane = slice(g * HEAD_DIM, (g + 1) * HEAD_DIM)
        parts = []
        for r in range(block):
            for s in range(steps):
                start = g * sharing * rows + r * steps + s
                parts.append(query_scratch[pl.ds(start, sharing, stride=rows), :])
        q = jnp.concatenate(parts, axis=0).astype(BF16)
        fresh = contract(q, new_k[:, lane], 1, 1) * scaling
        fresh = jnp.where(live_fresh, fresh, NEGATIVE)
        cached = []
        for r in range(block):
            score = contract(q[r * span : (r + 1) * span], cache_k[r, :, lane], 1, 1) * scaling
            cached.append(jnp.where(positions < lengths[step * block + r], score, NEGATIVE))
        cached = jnp.concatenate(cached, axis=0)
        top = jnp.maximum(
            jnp.max(cached, axis=1, keepdims=True), jnp.max(fresh, axis=1, keepdims=True)
        )
        cached = jnp.exp(cached - top)
        fresh = jnp.exp(fresh - top)
        total = jnp.sum(cached, axis=1, keepdims=True) + jnp.sum(fresh, axis=1, keepdims=True)
        cached = cached.astype(BF16)
        out = contract(fresh.astype(BF16), new_v[:, lane], 1, 0)
        out_cached = [
            contract(cached[r * span : (r + 1) * span], cache_v[r, :, lane], 1, 0)
            for r in range(block)
        ]
        out = (out + jnp.concatenate(out_cached, axis=0)) / total
        for r in range(block):
            for s in range(steps):
                start = g * sharing * total_rows + (step * block + r) * steps + s
                piece = out[r * span + s * sharing : r * span + (s + 1) * sharing]
                result_scratch[pl.ds(start, sharing, stride=total_rows), :] = piece

    @pl.when(step == pl.num_programs(0) - 1)
    def _():
        for h in range(heads):
            attended[:, h * HEAD_DIM : (h + 1) * HEAD_DIM] = result_scratch[
                h * total_rows : (h + 1) * total_rows, :
            ].astype(BF16)
        requests = total_rows // steps
        named = adapters[...]
        owner = lax.div(named, resident)
        local = named - owner * resident
        relative = jnp.bitwise_xor(owner, place[0])
        owner_id = lax.broadcasted_iota(jnp.int32, (owners, requests), 0)
        member = (owner_id == relative).astype(F32)
        before = lax.broadcasted_iota(jnp.int32, (requests, requests), 0) < (
            lax.broadcasted_iota(jnp.int32, (requests, requests), 1)
        )
        earlier = contract(member.astype(BF16), before.astype(BF16), 1, 0)
        slot = jnp.sum(earlier * member, axis=0, keepdims=True)
        facts = jnp.concatenate(
            [relative.astype(F32), slot, local.astype(F32), jnp.zeros((5, requests), F32)], axis=0
        )
        spread = lax.broadcasted_iota(jnp.int32, (requests, total_rows), 0) == lax.div(
            lax.broadcasted_iota(jnp.int32, (requests, total_rows), 1), steps
        )
        facts = contract(facts.astype(BF16), spread.astype(BF16), 1, 0).astype(jnp.int32)
        token = lax.rem(lax.broadcasted_iota(jnp.int32, (1, total_rows), 1), steps)
        target = (facts[0:1] * capacity + facts[1:2]) * steps + token
        slots = owners * capacity * steps
        placing = (
            lax.broadcasted_iota(jnp.int32, (slots, total_rows), 0) == target
        ).astype(BF16)
        placing_out[...] = placing
        chosen = (
            lax.broadcasted_iota(jnp.int32, (LANES, total_rows), 0) == facts[2:3]
        ).astype(BF16)
        per = capacity * steps
        marks = contract(placing, chosen, 1, 1).astype(BF16)
        tile = 512
        for c in range(0, width, tile):
            moved = contract(placing, attended[:, c : c + tile], 1, 0).astype(BF16)
            for k in range(owners):
                packed[k][:, c : c + tile] = moved[k * per : (k + 1) * per]
        for k in range(owners):
            packed[k][:, width:] = marks[k * per : (k + 1) * per]


def attend(queries, fresh_k, fresh_v, cache_k, cache_v, lengths, place, adapters, owners, resident):
    requests, steps, width = queries.shape
    cache_size, kv_width = cache_k.shape[1:]
    capacity = max(2, 2 * requests // owners)
    block = 8
    heads = width // HEAD_DIM
    total_rows = requests * steps
    per = capacity * steps
    whole = lambda shape: pl.BlockSpec(shape, lambda i, *_: (0,) * len(shape))
    return pl.pallas_call(
        functools.partial(attend_kernel, owners, resident, capacity),
        grid_spec=pltpu.PrefetchScalarGridSpec(
            num_scalar_prefetch=2,
            grid=(requests // block,),
            in_specs=[
                whole((1, requests)),
                pl.BlockSpec((block, steps, width), lambda i, *_: (i, 0, 0)),
                pl.BlockSpec((block, steps, kv_width), lambda i, *_: (i, 0, 0)),
                pl.BlockSpec((block, steps, kv_width), lambda i, *_: (i, 0, 0)),
                pl.BlockSpec((block, cache_size, kv_width), lambda i, *_: (i, 0, 0)),
                pl.BlockSpec((block, cache_size, kv_width), lambda i, *_: (i, 0, 0)),
            ],
            out_specs=[whole((total_rows, width)), whole((owners * per, total_rows))]
            + [whole((per, width + LANES))] * owners,
            scratch_shapes=[
                pltpu.VMEM((heads * block * steps, HEAD_DIM), F32),
                pltpu.VMEM((heads * total_rows, HEAD_DIM), F32),
            ],
        ),
        out_shape=[
            jax.ShapeDtypeStruct((total_rows, width), BF16),
            jax.ShapeDtypeStruct((owners * per, total_rows), BF16),
        ]
        + [jax.ShapeDtypeStruct((per, width + LANES), BF16)] * owners,
        compiler_params=pltpu.CompilerParams(vmem_limit_bytes=VMEM_LIMIT),
        cost_estimate=pl.CostEstimate(
            flops=8 * total_rows * width * cache_size,
            bytes_accessed=4 * requests * cache_size * kv_width,
            transcendentals=0,
        ),
        name="attend",
    )(lengths, place, adapters.reshape(1, requests), queries, fresh_k, fresh_v, cache_k, cache_v)


def project_kernel(column, attended, weight, out):
    out[...] = contract(attended[...], weight[...], 1, 0).astype(BF16)


def project(attended, weight, column, tile, blocks):
    rows, depth = attended.shape
    columns = weight.shape[1] // blocks
    tiles = columns // tile
    return pl.pallas_call(
        project_kernel,
        grid_spec=pltpu.PrefetchScalarGridSpec(
            num_scalar_prefetch=1,
            grid=(tiles,),
            in_specs=[
                pl.BlockSpec((rows, depth), lambda i, c: (0, 0)),
                pl.BlockSpec((depth, tile), lambda i, c: (0, c[0] * tiles + i)),
            ],
            out_specs=pl.BlockSpec((rows, tile), lambda i, c: (0, i)),
        ),
        out_shape=jax.ShapeDtypeStruct((rows, columns), BF16),
        compiler_params=pltpu.CompilerParams(vmem_limit_bytes=VMEM_LIMIT),
        cost_estimate=pl.CostEstimate(
            flops=2 * rows * depth * columns,
            bytes_accessed=2 * depth * columns,
            transcendentals=0,
        ),
        name="project",
    )(column, attended, weight)


def low_kernel(owners, resident, down, *refs):
    packed = refs[:owners]
    low_out, marks_out = refs[owners:]
    depth = down.shape[1]
    rank = down.shape[0] // resident
    per = packed[0].shape[0]
    weight = down[...]
    lows = []
    for k in range(owners):
        every = contract(packed[k][:, :depth], weight, 1, 1)
        marks = packed[k][:, depth:]
        marks_out[k * per : (k + 1) * per, :] = marks
        marks = marks.astype(F32)
        low = every[:, :rank] * marks[:, 0:1]
        for y in range(1, resident):
            low = low + every[:, y * rank : (y + 1) * rank] * marks[:, y : y + 1]
        lows.append(low)
    half = owners // 2
    low_out[...] = jnp.concatenate(
        [jnp.concatenate(lows[:half], axis=0), jnp.concatenate(lows[half:], axis=0)], axis=1
    ).astype(BF16)


def low_partial(packed, down, owners):
    resident, rank, depth = down.shape
    per = packed[0].shape[0]
    slots = owners * per
    return pl.pallas_call(
        functools.partial(low_kernel, owners, resident),
        out_shape=[
            jax.ShapeDtypeStruct((slots // 2, 2 * rank), BF16),
            jax.ShapeDtypeStruct((slots, LANES), BF16),
        ],
        compiler_params=pltpu.CompilerParams(vmem_limit_bytes=VMEM_LIMIT),
        cost_estimate=pl.CostEstimate(
            flops=2 * slots * depth * resident * rank,
            bytes_accessed=2 * depth * resident * rank,
            transcendentals=0,
        ),
        name="low",
    )(down.reshape(resident * rank, depth), *packed)


def delta_kernel(owners, resident, marks, up, *refs):
    outs = refs[len(refs) - owners :]
    partials = refs[: len(refs) - owners]
    low = partials[0][...].astype(F32)
    for part in partials[1:]:
        low = low + part[...].astype(F32)
    rank = low.shape[1] // 2
    low = low.astype(BF16).astype(F32)
    low = jnp.concatenate([low[:, :rank], low[:, rank:]], axis=0)
    chosen = marks[...].astype(F32)
    spread = jnp.concatenate(
        [low * chosen[:, y : y + 1] for y in range(resident)], axis=1
    ).astype(BF16)
    answer = contract(spread, up[...], 1, 0).astype(BF16)
    per = answer.shape[0] // owners
    for k in range(owners):
        outs[k][...] = answer[k * per : (k + 1) * per]


def delta(marks, up, partials, owners):
    resident, rank, columns = up.shape
    slots = marks.shape[0]
    return pl.pallas_call(
        functools.partial(delta_kernel, owners, resident),
        out_shape=[jax.ShapeDtypeStruct((slots // owners, columns), BF16)] * owners,
        compiler_params=pltpu.CompilerParams(vmem_limit_bytes=VMEM_LIMIT),
        cost_estimate=pl.CostEstimate(
            flops=2 * slots * columns * resident * rank,
            bytes_accessed=2 * columns * resident * rank,
            transcendentals=0,
        ),
        name="delta",
    )(marks, up.reshape(resident * rank, columns), *partials)


def combine_kernel(owners, placing, *refs):
    answers = refs[:owners]
    partials = refs[owners:-1]
    out = refs[-1]
    base = partials[0][...].astype(F32)
    for part in partials[1:]:
        base = base + part[...].astype(F32)
    answer = jnp.concatenate([a[...] for a in answers], axis=0)
    base = base + contract(placing[...], answer, 0, 0)
    out[...] = base.astype(BF16)


def combine(placing, answers, partials):
    rows, columns = partials[0].shape
    return pl.pallas_call(
        functools.partial(combine_kernel, len(answers)),
        out_shape=jax.ShapeDtypeStruct((rows, columns), BF16),
        compiler_params=pltpu.CompilerParams(vmem_limit_bytes=VMEM_LIMIT),
        name="combine",
    )(placing, *answers, *partials)


def swap(value, axis, k):
    count = lax.axis_size(axis)
    return lax.ppermute(value, axis, [(i, i ^ k) for i in range(count)])


def body(
    queries,
    token_key_rows,
    token_value_rows,
    cached_key_rows,
    cached_value_rows,
    cache_length,
    request_adapter,
    output_weight_matrix,
    adapter_down_weight,
    adapter_up_weight,
):
    requests, steps, _ = queries.shape
    owners = lax.axis_size("adapter")
    blocks = lax.axis_size("tensor")
    resident = adapter_down_weight.shape[0]
    place = lax.axis_index("adapter").reshape(1)
    mine = lax.axis_index("tensor")

    attended, placing, *packed = attend(
        queries,
        token_key_rows,
        token_value_rows,
        cached_key_rows,
        cached_value_rows,
        cache_length,
        place,
        request_adapter,
        owners,
        resident,
    )
    columns = output_weight_matrix.shape[1] // blocks
    tile = min(512, columns)
    far_first = list(range(blocks - 1, 0, -1))
    partials = {}
    for k in far_first:
        column = jnp.bitwise_xor(mine, k).reshape(1)
        partials[k] = swap(
            project(attended, output_weight_matrix, column, tile, blocks), "tensor", k
        )
    arrived = {0: packed[0]}
    for k in range(owners - 1, 0, -1):
        arrived[k] = swap(packed[k], "adapter", k)
    own = project(attended, output_weight_matrix, mine.reshape(1), tile, blocks)
    low, marks = low_partial([arrived[k] for k in range(owners)], adapter_down_weight, owners)
    lows = [low] + [swap(low, "tensor", k) for k in far_first]
    answers = delta(marks, adapter_up_weight, lows, owners)
    returned = [answers[0]] + [None] * (owners - 1)
    for k in range(owners - 1, 0, -1):
        returned[k] = swap(answers[k], "adapter", k)
    mixed = combine(placing, returned, [own] + [partials[k] for k in far_first])
    return mixed.reshape(requests, steps, columns)


def solution(mesh):
    rows = P(("group", "adapter"), None, "tensor")
    return jax.shard_map(
        body,
        mesh=mesh,
        in_specs=(
            rows,
            rows,
            rows,
            rows,
            rows,
            P(("group", "adapter")),
            P(("group", "adapter")),
            P("tensor", None),
            rows,
            rows,
        ),
        out_specs=rows,
        check_vma=False,
    )
```

```python
import functools
import math

import jax
import jax.numpy as jnp
from jax import lax
from jax.experimental import pallas as pl
from jax.experimental.pallas import tpu as pltpu
from jax.sharding import PartitionSpec as P

HEAD_DIM = 128
NEGATIVE = -1e30
LANES = 128
KERNEL_VMEM = 32 * 1024 * 1024
SMALL_VMEM = 12 * 1024 * 1024

F32 = jnp.float32
BF16 = jnp.bfloat16


def contract(a, b, a_dim, b_dim):
    return lax.dot_general(
        a, b, (((a_dim,), (b_dim,)), ((), ())), preferred_element_type=F32
    )


def attend_kernel(
    owners,
    resident,
    capacity,
    block,
    lengths,
    place,
    column,
    adapters,
    queries_hbm,
    fresh_k_hbm,
    fresh_v_hbm,
    cache_k_hbm,
    cache_v_hbm,
    weight_hbm,
    *rest,
):
    attended_hbm, placing_hbm, marks_hbm, partial_hbm = rest[:4]
    packed_hbm = rest[4 : 4 + owners]
    (
        queries,
        fresh_k,
        fresh_v,
        cache_k,
        cache_v,
        weight,
        new_k,
        new_v,
        query_scratch,
        result_scratch,
        attended,
        placing_out,
        marks_out,
        partial,
        packed,
        small_sem,
        cache_sem,
        weight_sem,
        out_sem,
    ) = rest[4 + owners :]
    requests, steps, width = queries.shape
    heads = width // HEAD_DIM
    groups = cache_k.shape[2] // HEAD_DIM
    sharing = heads // groups
    cache_size = cache_k.shape[1]
    rows = block * steps
    total_rows = requests * steps
    span = steps * sharing
    chunks = requests // block
    columns = partial.shape[1]

    def cache_copies(i):
        part = pl.ds(i * block, block)
        return (
            pltpu.make_async_copy(cache_k_hbm.at[part], cache_k.at[part], cache_sem.at[0, i]),
            pltpu.make_async_copy(cache_v_hbm.at[part], cache_v.at[part], cache_sem.at[1, i]),
        )

    small = [
        pltpu.make_async_copy(queries_hbm, queries, small_sem.at[0]),
        pltpu.make_async_copy(fresh_k_hbm, fresh_k, small_sem.at[1]),
        pltpu.make_async_copy(fresh_v_hbm, fresh_v, small_sem.at[2]),
    ]
    for copy in small:
        copy.start()
    for i in range(chunks):
        for copy in cache_copies(i):
            copy.start()
    weight_copy = pltpu.make_async_copy(
        weight_hbm.at[:, pl.ds(pl.multiple_of(column[0] * columns, LANES), columns)],
        weight,
        weight_sem.at[0],
    )
    weight_copy.start()

    named = adapters[...]
    owner = lax.div(named, resident)
    local = named - owner * resident
    relative = jnp.bitwise_xor(owner, place[0])
    owner_id = lax.broadcasted_iota(jnp.int32, (owners, requests), 0)
    member = (owner_id == relative).astype(F32)
    before = lax.broadcasted_iota(jnp.int32, (requests, requests), 0) < (
        lax.broadcasted_iota(jnp.int32, (requests, requests), 1)
    )
    earlier = contract(member.astype(BF16), before.astype(BF16), 1, 0)
    slot = jnp.sum(earlier * member, axis=0, keepdims=True)
    facts = jnp.concatenate(
        [relative.astype(F32), slot, local.astype(F32), jnp.zeros((5, requests), F32)], axis=0
    )
    spread = lax.broadcasted_iota(jnp.int32, (requests, total_rows), 0) == lax.div(
        lax.broadcasted_iota(jnp.int32, (requests, total_rows), 1), steps
    )
    facts = contract(facts.astype(BF16), spread.astype(BF16), 1, 0).astype(jnp.int32)
    token = lax.rem(lax.broadcasted_iota(jnp.int32, (1, total_rows), 1), steps)
    target = (facts[0:1] * capacity + facts[1:2]) * steps + token
    slots = owners * capacity * steps
    placing = (
        lax.broadcasted_iota(jnp.int32, (slots, total_rows), 0) == target
    ).astype(BF16)
    placing_out[...] = placing
    chosen = (
        lax.broadcasted_iota(jnp.int32, (LANES, total_rows), 0) == facts[2:3]
    ).astype(BF16)
    packed[:, width:] = contract(placing, chosen, 1, 1).astype(BF16)
    adapter_id = lax.broadcasted_iota(jnp.int32, (LANES, total_rows), 0)
    named_here = (adapter_id == facts[0:1] * resident + facts[2:3]).astype(BF16)
    identity = lax.broadcasted_iota(jnp.int32, (total_rows, total_rows), 0) == (
        lax.broadcasted_iota(jnp.int32, (total_rows, total_rows), 1)
    )
    marks_out[...] = contract(identity.astype(BF16), named_here, 1, 1).astype(BF16)

    positions = lax.broadcasted_iota(jnp.int32, (groups * span, cache_size), 1)
    row_id = lax.broadcasted_iota(jnp.int32, (block * groups * span, total_rows), 0)
    col_id = lax.broadcasted_iota(jnp.int32, (block * groups * span, total_rows), 1)
    distance = lax.div(row_id, groups * span) - lax.div(col_id, steps)
    causal = lax.rem(col_id, steps) <= lax.div(lax.rem(row_id, span), sharing)
    distance = jnp.where(causal, distance, requests)
    scaling = math.log2(math.e) / math.sqrt(HEAD_DIM)
    for copy in small:
        copy.wait()
    new_k[...] = fresh_k[...].reshape(total_rows, groups * HEAD_DIM)
    new_v[...] = fresh_v[...].reshape(total_rows, groups * HEAD_DIM)

    @pl.loop(0, chunks)
    def _(i):
        base = i * block
        flat = queries[pl.ds(base, block)].astype(F32).reshape(rows, width)
        for h in range(heads):
            query_scratch[h * rows : (h + 1) * rows, :] = flat[
                :, h * HEAD_DIM : (h + 1) * HEAD_DIM
            ]
        for copy in cache_copies(i):
            copy.wait()
        live_fresh = distance == -base
        empty = jnp.zeros((span, HEAD_DIM), BF16)
        wide = []
        for r in range(block):
            for g in range(groups):
                parts = []
                for s in range(steps):
                    start = g * sharing * rows + r * steps + s
                    parts.append(query_scratch[pl.ds(start, sharing, stride=rows), :])
                q = jnp.concatenate(parts, axis=0).astype(BF16)
                wide.append(
                    jnp.concatenate([q if o == g else empty for o in range(groups)], axis=1)
                )
        q = jnp.concatenate(wide, axis=0)
        fresh = jnp.where(live_fresh, contract(q, new_k[...], 1, 1), NEGATIVE)
        band = groups * span
        cached = []
        for r in range(block):
            score = contract(q[r * band : (r + 1) * band], cache_k[base + r], 1, 1)
            cached.append(jnp.where(positions < lengths[base + r], score, NEGATIVE))
        cached = jnp.concatenate(cached, axis=0)
        top = jnp.max(jnp.maximum(cached, fresh), axis=1, keepdims=True)
        cached = jnp.exp2((cached - top) * scaling)
        fresh = jnp.exp2((fresh - top) * scaling)
        scale = 1.0 / jnp.sum(cached + fresh, axis=1, keepdims=True)
        cached = cached.astype(BF16)
        out = contract(fresh.astype(BF16), new_v[...], 1, 0)
        for r in range(block):
            rows_r = slice(r * band, (r + 1) * band)
            both = (
                contract(cached[rows_r], cache_v[base + r], 1, 0) + out[rows_r]
            )
            for g in range(groups):
                for s in range(steps):
                    first = g * span + s * sharing
                    piece = both[
                        first : first + sharing, g * HEAD_DIM : (g + 1) * HEAD_DIM
                    ] * scale[r * band + first : r * band + first + sharing]
                    start = g * sharing * total_rows + (base + r) * steps + s
                    result_scratch[pl.ds(start, sharing, stride=total_rows), :] = piece

    for h in range(heads):
        attended[:, h * HEAD_DIM : (h + 1) * HEAD_DIM] = result_scratch[
            h * total_rows : (h + 1) * total_rows, :
        ].astype(BF16)
    attended_copy = pltpu.make_async_copy(attended, attended_hbm, out_sem.at[0])
    attended_copy.start()
    placing_copy = pltpu.make_async_copy(placing_out, placing_hbm, out_sem.at[1])
    placing_copy.start()
    marks_copy = pltpu.make_async_copy(marks_out, marks_hbm, out_sem.at[2])
    marks_copy.start()
    per = capacity * steps
    tile = min(512, width)
    for c in range(0, width, tile):
        packed[:, c : c + tile] = contract(
            placing_out[...], attended[:, c : c + tile], 1, 0
        ).astype(BF16)
    packed_copies = [
        pltpu.make_async_copy(
            packed.at[pl.ds(k * per, per)], packed_hbm[k], out_sem.at[4 + k]
        )
        for k in range(owners)
    ]
    for copy in packed_copies:
        copy.start()
    weight_copy.wait()
    tile = min(256, columns)
    for c in range(0, columns, tile):
        partial[:, c : c + tile] = contract(
            attended[...], weight[:, c : c + tile], 1, 0
        ).astype(BF16)
    partial_copy = pltpu.make_async_copy(partial, partial_hbm, out_sem.at[3])
    partial_copy.start()
    attended_copy.wait()
    placing_copy.wait()
    marks_copy.wait()
    for copy in packed_copies:
        copy.wait()
    partial_copy.wait()


def attend(
    queries,
    fresh_k,
    fresh_v,
    cache_k,
    cache_v,
    weight,
    lengths,
    place,
    column,
    adapters,
    owners,
    resident,
    columns,
):
    requests, steps, width = queries.shape
    cache_size, kv_width = cache_k.shape[1:]
    capacity = max(2, 2 * requests // owners)
    block = min(32, requests)
    heads = width // HEAD_DIM
    total_rows = requests * steps
    per = capacity * steps
    anywhere = pl.BlockSpec(memory_space=pl.ANY)
    return pl.pallas_call(
        functools.partial(attend_kernel, owners, resident, capacity, block),
        grid_spec=pltpu.PrefetchScalarGridSpec(
            num_scalar_prefetch=3,
            grid=(1,),
            in_specs=[pl.BlockSpec((1, requests), lambda i, *_: (0, 0))] + [anywhere] * 6,
            out_specs=[anywhere] * (4 + owners),
            scratch_shapes=[
                pltpu.VMEM((requests, steps, width), BF16),
                pltpu.VMEM((requests, steps, kv_width), BF16),
                pltpu.VMEM((requests, steps, kv_width), BF16),
                pltpu.VMEM((requests, cache_size, kv_width), BF16),
                pltpu.VMEM((requests, cache_size, kv_width), BF16),
                pltpu.VMEM((width, columns), BF16),
                pltpu.VMEM((total_rows, kv_width), BF16),
                pltpu.VMEM((total_rows, kv_width), BF16),
                pltpu.VMEM((heads * block * steps, HEAD_DIM), F32),
                pltpu.VMEM((heads * total_rows, HEAD_DIM), F32),
                pltpu.VMEM((total_rows, width), BF16),
                pltpu.VMEM((owners * per, total_rows), BF16),
                pltpu.VMEM((total_rows, LANES), BF16),
                pltpu.VMEM((total_rows, columns), BF16),
                pltpu.VMEM((owners * per, width + LANES), BF16),
                pltpu.SemaphoreType.DMA((3,)),
                pltpu.SemaphoreType.DMA((2, requests // block)),
                pltpu.SemaphoreType.DMA((1,)),
                pltpu.SemaphoreType.DMA((4 + owners,)),
            ],
        ),
        out_shape=[
            jax.ShapeDtypeStruct((total_rows, width), BF16),
            jax.ShapeDtypeStruct((owners * per, total_rows), BF16),
            jax.ShapeDtypeStruct((total_rows, LANES), BF16),
            jax.ShapeDtypeStruct((total_rows, columns), BF16),
        ]
        + [jax.ShapeDtypeStruct((per, width + LANES), BF16)] * owners,
        compiler_params=pltpu.CompilerParams(vmem_limit_bytes=KERNEL_VMEM),
        cost_estimate=pl.CostEstimate(
            flops=8 * total_rows * width * cache_size,
            bytes_accessed=4 * requests * cache_size * kv_width,
            transcendentals=0,
        ),
        name="attend",
    )(
        lengths,
        place,
        column,
        adapters.reshape(1, requests),
        queries,
        fresh_k,
        fresh_v,
        cache_k,
        cache_v,
        weight,
    )


def project_kernel(count, *refs):
    places = refs[:count]
    attended_hbm, weight_hbm = refs[count : count + 2]
    outs = refs[count + 2 : 2 * count + 2]
    attended, weight, results, in_sem, weight_sem, out_sem = refs[2 * count + 2 :]
    columns = results.shape[2]
    attended_copy = pltpu.make_async_copy(attended_hbm, attended, in_sem.at[0])
    attended_copy.start()
    copies = []
    for j in range(count):
        start = pl.multiple_of(places[j][0] * columns, LANES)
        copy = pltpu.make_async_copy(
            weight_hbm.at[:, pl.ds(start, columns)], weight.at[j], weight_sem.at[j]
        )
        copy.start()
        copies.append(copy)
    attended_copy.wait()
    tile = min(256, columns)
    writes = []
    for j in range(count):
        copies[j].wait()
        for c in range(0, columns, tile):
            results[j, :, c : c + tile] = contract(
                attended[...], weight[j, :, c : c + tile], 1, 0
            ).astype(BF16)
        write = pltpu.make_async_copy(results.at[j], outs[j], out_sem.at[j])
        write.start()
        writes.append(write)
    for write in writes:
        write.wait()


def project(attended, weight, places, blocks):
    rows, depth = attended.shape
    columns = weight.shape[1] // blocks
    count = len(places)
    anywhere = pl.BlockSpec(memory_space=pl.ANY)
    return pl.pallas_call(
        functools.partial(project_kernel, count),
        grid_spec=pltpu.PrefetchScalarGridSpec(
            num_scalar_prefetch=count,
            grid=(1,),
            in_specs=[anywhere] * 2,
            out_specs=[anywhere] * count,
            scratch_shapes=[
                pltpu.VMEM((rows, depth), BF16),
                pltpu.VMEM((count, depth, columns), BF16),
                pltpu.VMEM((count, rows, columns), BF16),
                pltpu.SemaphoreType.DMA((1,)),
                pltpu.SemaphoreType.DMA((count,)),
                pltpu.SemaphoreType.DMA((count,)),
            ],
        ),
        out_shape=[jax.ShapeDtypeStruct((rows, columns), BF16)] * count,
        compiler_params=pltpu.CompilerParams(vmem_limit_bytes=KERNEL_VMEM),
        cost_estimate=pl.CostEstimate(
            flops=2 * rows * depth * columns * count,
            bytes_accessed=2 * depth * columns * count,
            transcendentals=0,
        ),
        name="project",
    )(*places, attended, weight)


def low_kernel(owners, resident, down, *refs):
    packed = refs[:owners]
    outs = refs[owners:]
    depth = down.shape[1]
    rank = down.shape[0] // resident
    weight = down[...]
    for k in range(owners):
        every = contract(packed[k][:, :depth], weight, 1, 1)
        marks = packed[k][:, depth:].astype(F32)
        low = every[:, :rank] * marks[:, 0:1]
        for y in range(1, resident):
            low = low + every[:, y * rank : (y + 1) * rank] * marks[:, y : y + 1]
        outs[k][...] = jnp.concatenate([low, jnp.zeros_like(low)], axis=1).astype(BF16)


def low_partial(packed, down):
    resident, rank, depth = down.shape
    owners = len(packed)
    per = packed[0].shape[0]
    return pl.pallas_call(
        functools.partial(low_kernel, owners, resident),
        out_shape=[jax.ShapeDtypeStruct((per, 2 * rank), BF16)] * owners,
        compiler_params=pltpu.CompilerParams(vmem_limit_bytes=SMALL_VMEM),
        cost_estimate=pl.CostEstimate(
            flops=2 * owners * per * depth * resident * rank,
            bytes_accessed=2 * depth * resident * rank,
            transcendentals=0,
        ),
        name="low",
    )(down.reshape(resident * rank, depth), *packed)


def unpack_kernel(placing, *refs):
    out = refs[-1]
    slots = jnp.concatenate([part[...] for part in refs[:-1]], axis=0)
    low = contract(placing[...], slots, 0, 0)
    half = low.shape[0] // 2
    rank = low.shape[1] // 2
    out[...] = jnp.concatenate([low[:half, :rank], low[half:, :rank]], axis=1).astype(BF16)


def unpack(placing, slots):
    rows = placing.shape[1]
    return pl.pallas_call(
        unpack_kernel,
        out_shape=jax.ShapeDtypeStruct((rows // 2, slots[0].shape[1]), BF16),
        compiler_params=pltpu.CompilerParams(vmem_limit_bytes=SMALL_VMEM),
        cost_estimate=pl.CostEstimate(flops=2**20, bytes_accessed=2**18, transcendentals=0),
        name="unpack",
    )(placing, *slots)


def combine_kernel(blocks, resident, marks, *refs):
    partials = refs[:blocks]
    lows = refs[blocks : 2 * blocks]
    ups = refs[2 * blocks : -1]
    out = refs[-1]
    base = partials[0][...].astype(F32)
    low = lows[0][...].astype(F32)
    for part in partials[1:]:
        base = base + part[...].astype(F32)
    for part in lows[1:]:
        low = low + part[...].astype(F32)
    rank = low.shape[1] // 2
    low = low.astype(BF16).astype(F32)
    low = jnp.concatenate([low[:, :rank], low[:, rank:]], axis=0)
    chosen = marks[...].astype(F32)
    first = 0
    for up in ups:
        held = up.shape[0] // rank
        spread = jnp.concatenate(
            [low * chosen[:, y : y + 1] for y in range(first, first + held)], axis=1
        ).astype(BF16)
        base = base + contract(spread, up[...], 1, 0)
        first += held
    out[...] = base.reshape(out.shape).astype(BF16)


def combine(marks, partials, lows, ups, resident, steps):
    rows, columns = partials[0].shape
    return pl.pallas_call(
        functools.partial(combine_kernel, len(partials), resident),
        out_shape=jax.ShapeDtypeStruct((rows // steps, steps, columns), BF16),
        compiler_params=pltpu.CompilerParams(vmem_limit_bytes=SMALL_VMEM),
        cost_estimate=pl.CostEstimate(flops=2**28, bytes_accessed=2**22, transcendentals=0),
        name="combine",
    )(marks, *partials, *lows, *ups)


def swap(value, axis, k):
    count = lax.axis_size(axis)
    return lax.ppermute(value, axis, [(i, i ^ k) for i in range(count)])


def gather(value, axis):
    held = {0: value}
    bit = lax.axis_size(axis) // 2
    while bit:
        for k in list(held):
            held[k ^ bit] = swap(held[k], axis, bit)
        bit //= 2
    return held


def body(
    queries,
    token_key_rows,
    token_value_rows,
    cached_key_rows,
    cached_value_rows,
    cache_length,
    request_adapter,
    output_weight_matrix,
    adapter_down_weight,
    adapter_up_weight,
):
    requests, steps, _ = queries.shape
    owners = lax.axis_size("adapter")
    blocks = lax.axis_size("tensor")
    resident, rank, columns = adapter_up_weight.shape
    place = lax.axis_index("adapter").reshape(1)
    mine = lax.axis_index("tensor")
    columns_of = lambda k: jnp.bitwise_xor(mine, k).reshape(1)

    up_rows = adapter_up_weight.reshape(resident * rank, columns)
    cut = resident * rank // 2
    early, late = up_rows[:cut], up_rows[cut:]
    early_parts = gather(early, "adapter")

    far = blocks - 1
    attended, placing, marks, first_partial, *packed = attend(
        queries,
        token_key_rows,
        token_value_rows,
        cached_key_rows,
        cached_value_rows,
        output_weight_matrix,
        cache_length,
        place,
        columns_of(far),
        request_adapter,
        owners,
        resident,
        columns,
    )
    arrived = [packed[0]] + [None] * (owners - 1)
    for k in range(owners - 1, 0, -1):
        arrived[k] = swap(packed[k], "adapter", k)
    partials = {far: swap(first_partial, "tensor", far)}
    others = list(range(far - 1, 0, -1))
    made = project(attended, output_weight_matrix, [columns_of(k) for k in others], blocks)
    for k, part in zip(others, made):
        partials[k] = swap(part, "tensor", k)
    (own,) = project(attended, output_weight_matrix, [mine.reshape(1)], blocks)
    lows = low_partial(arrived, adapter_down_weight)
    returned = [lows[0]] + [swap(lows[k], "adapter", k) for k in range(1, owners)]
    late, _ = lax.optimization_barrier((late, lows[1]))
    late_parts = gather(late, "adapter")
    low = unpack(placing, returned)
    low_parts = [low] + [swap(low, "tensor", k) for k in range(1, blocks)]
    ups = []
    for k in range(owners):
        ups += [early_parts[k], late_parts[k]]
    return combine(
        marks,
        [own] + [partials[k] for k in range(1, blocks)],
        low_parts,
        ups,
        resident,
        steps,
    )


def solution(mesh):
    rows = P(("group", "adapter"), None, "tensor")
    return jax.shard_map(
        body,
        mesh=mesh,
        in_specs=(
            rows,
            rows,
            rows,
            rows,
            rows,
            P(("group", "adapter")),
            P(("group", "adapter")),
            P("tensor", None),
            rows,
            rows,
        ),
        out_specs=rows,
        check_vma=False,
    )
```

```python
import functools
import math

import jax
import jax.numpy as jnp
from jax import lax
from jax.experimental import pallas as pl
from jax.experimental.pallas import tpu as pltpu
from jax.sharding import PartitionSpec as P

HEAD_DIM = 128
NEGATIVE = -1e30
LANES = 128
KERNEL_VMEM = 56 * 1024 * 1024
SMALL_COST = pl.CostEstimate(flops=1024, bytes_accessed=1024, transcendentals=0)
SMALL_VMEM = 12 * 1024 * 1024

F32 = jnp.float32
BF16 = jnp.bfloat16


def contract(a, b, a_dim, b_dim):
    return lax.dot_general(
        a, b, (((a_dim,), (b_dim,)), ((), ())), preferred_element_type=F32
    )


def attend_kernel(
    owners,
    resident,
    capacity,
    block,
    lengths,
    place,
    column,
    adapters,
    queries_hbm,
    fresh_k_hbm,
    fresh_v_hbm,
    cache_k_hbm,
    cache_v_hbm,
    weight_hbm,
    *rest,
):
    attended_hbm, placing_hbm, marks_hbm, partial_hbm = rest[:4]
    packed_hbm = rest[4 : 4 + owners]
    (
        queries,
        fresh_k,
        fresh_v,
        cache_k,
        cache_v,
        weight,
        new_k,
        new_v,
        query_scratch,
        result_scratch,
        attended,
        placing_out,
        marks_out,
        partial,
        packed,
        small_sem,
        cache_sem,
        weight_sem,
        out_sem,
    ) = rest[4 + owners :]
    requests, steps, width = queries.shape
    heads = width // HEAD_DIM
    groups = cache_k.shape[2] // HEAD_DIM
    sharing = heads // groups
    cache_size = cache_k.shape[1]
    rows = block * steps
    total_rows = requests * steps
    span = steps * sharing
    chunks = requests // block
    columns = partial.shape[1]

    def cache_copies(i):
        part = pl.ds(i * block, block)
        return (
            pltpu.make_async_copy(cache_k_hbm.at[part], cache_k.at[part], cache_sem.at[0, i]),
            pltpu.make_async_copy(cache_v_hbm.at[part], cache_v.at[part], cache_sem.at[1, i]),
        )

    small = [
        pltpu.make_async_copy(queries_hbm, queries, small_sem.at[0]),
        pltpu.make_async_copy(fresh_k_hbm, fresh_k, small_sem.at[1]),
        pltpu.make_async_copy(fresh_v_hbm, fresh_v, small_sem.at[2]),
    ]
    for copy in small:
        copy.start()
    for i in range(chunks):
        for copy in cache_copies(i):
            copy.start()
    weight_copy = pltpu.make_async_copy(
        weight_hbm.at[:, pl.ds(pl.multiple_of(column[0] * columns, LANES), columns)],
        weight,
        weight_sem.at[0],
    )
    weight_copy.start()

    named = adapters[...]
    owner = lax.div(named, resident)
    local = named - owner * resident
    relative = jnp.bitwise_xor(owner, place[0])
    owner_id = lax.broadcasted_iota(jnp.int32, (owners, requests), 0)
    member = (owner_id == relative).astype(F32)
    before = lax.broadcasted_iota(jnp.int32, (requests, requests), 0) < (
        lax.broadcasted_iota(jnp.int32, (requests, requests), 1)
    )
    earlier = contract(member.astype(BF16), before.astype(BF16), 1, 0)
    slot = jnp.sum(earlier * member, axis=0, keepdims=True)
    facts = jnp.concatenate(
        [relative.astype(F32), slot, local.astype(F32), jnp.zeros((5, requests), F32)], axis=0
    )
    spread = lax.broadcasted_iota(jnp.int32, (requests, total_rows), 0) == lax.div(
        lax.broadcasted_iota(jnp.int32, (requests, total_rows), 1), steps
    )
    facts = contract(facts.astype(BF16), spread.astype(BF16), 1, 0).astype(jnp.int32)
    token = lax.rem(lax.broadcasted_iota(jnp.int32, (1, total_rows), 1), steps)
    target = (facts[0:1] * capacity + facts[1:2]) * steps + token
    slots = owners * capacity * steps
    placing = (
        lax.broadcasted_iota(jnp.int32, (slots, total_rows), 0) == target
    ).astype(BF16)
    placing_out[...] = placing
    chosen = (
        lax.broadcasted_iota(jnp.int32, (LANES, total_rows), 0) == facts[2:3]
    ).astype(BF16)
    packed[:, width:] = contract(placing, chosen, 1, 1).astype(BF16)
    adapter_id = lax.broadcasted_iota(jnp.int32, (LANES, total_rows), 0)
    named_here = (adapter_id == facts[0:1] * resident + facts[2:3]).astype(BF16)
    identity = lax.broadcasted_iota(jnp.int32, (total_rows, total_rows), 0) == (
        lax.broadcasted_iota(jnp.int32, (total_rows, total_rows), 1)
    )
    marks_out[...] = contract(identity.astype(BF16), named_here, 1, 1).astype(BF16)

    positions = lax.broadcasted_iota(jnp.int32, (groups * span, cache_size), 1)
    row_id = lax.broadcasted_iota(jnp.int32, (block * groups * span, total_rows), 0)
    col_id = lax.broadcasted_iota(jnp.int32, (block * groups * span, total_rows), 1)
    distance = lax.div(row_id, groups * span) - lax.div(col_id, steps)
    causal = lax.rem(col_id, steps) <= lax.div(lax.rem(row_id, span), sharing)
    distance = jnp.where(causal, distance, requests)
    scaling = math.log2(math.e) / math.sqrt(HEAD_DIM)
    for copy in small:
        copy.wait()
    new_k[...] = fresh_k[...].reshape(total_rows, groups * HEAD_DIM)
    new_v[...] = fresh_v[...].reshape(total_rows, groups * HEAD_DIM)

    @pl.loop(0, chunks)
    def _(i):
        base = i * block
        flat = queries[pl.ds(base, block)].astype(F32).reshape(rows, width)
        for h in range(heads):
            query_scratch[h * rows : (h + 1) * rows, :] = flat[
                :, h * HEAD_DIM : (h + 1) * HEAD_DIM
            ]
        for copy in cache_copies(i):
            copy.wait()
        live_fresh = distance == -base
        empty = jnp.zeros((span, HEAD_DIM), BF16)
        wide = []
        for r in range(block):
            for g in range(groups):
                parts = []
                for s in range(steps):
                    start = g * sharing * rows + r * steps + s
                    parts.append(query_scratch[pl.ds(start, sharing, stride=rows), :])
                q = jnp.concatenate(parts, axis=0).astype(BF16)
                wide.append(
                    jnp.concatenate([q if o == g else empty for o in range(groups)], axis=1)
                )
        q = jnp.concatenate(wide, axis=0)
        fresh = jnp.where(live_fresh, contract(q, new_k[...], 1, 1), NEGATIVE)
        band = groups * span
        cached = []
        for r in range(block):
            score = contract(q[r * band : (r + 1) * band], cache_k[base + r], 1, 1)
            cached.append(jnp.where(positions < lengths[base + r], score, NEGATIVE))
        cached = jnp.concatenate(cached, axis=0)
        top = jnp.max(jnp.maximum(cached, fresh), axis=1, keepdims=True)
        cached = jnp.exp2((cached - top) * scaling)
        fresh = jnp.exp2((fresh - top) * scaling)
        scale = 1.0 / jnp.sum(cached + fresh, axis=1, keepdims=True)
        cached = cached.astype(BF16)
        out = contract(fresh.astype(BF16), new_v[...], 1, 0)
        for r in range(block):
            rows_r = slice(r * band, (r + 1) * band)
            both = (
                contract(cached[rows_r], cache_v[base + r], 1, 0) + out[rows_r]
            )
            for g in range(groups):
                for s in range(steps):
                    first = g * span + s * sharing
                    piece = both[
                        first : first + sharing, g * HEAD_DIM : (g + 1) * HEAD_DIM
                    ] * scale[r * band + first : r * band + first + sharing]
                    start = g * sharing * total_rows + (base + r) * steps + s
                    result_scratch[pl.ds(start, sharing, stride=total_rows), :] = piece

    for h in range(heads):
        attended[:, h * HEAD_DIM : (h + 1) * HEAD_DIM] = result_scratch[
            h * total_rows : (h + 1) * total_rows, :
        ].astype(BF16)
    attended_copy = pltpu.make_async_copy(attended, attended_hbm, out_sem.at[0])
    attended_copy.start()
    placing_copy = pltpu.make_async_copy(placing_out, placing_hbm, out_sem.at[1])
    placing_copy.start()
    marks_copy = pltpu.make_async_copy(marks_out, marks_hbm, out_sem.at[2])
    marks_copy.start()
    per = capacity * steps
    tile = min(512, width)
    for c in range(0, width, tile):
        packed[:, c : c + tile] = contract(
            placing_out[...], attended[:, c : c + tile], 1, 0
        ).astype(BF16)
    packed_copies = [
        pltpu.make_async_copy(
            packed.at[pl.ds(k * per, per)], packed_hbm[k], out_sem.at[4 + k]
        )
        for k in range(owners)
    ]
    for copy in packed_copies:
        copy.start()
    weight_copy.wait()
    tile = min(256, columns)
    for c in range(0, columns, tile):
        partial[:, c : c + tile] = contract(
            attended[...], weight[:, c : c + tile], 1, 0
        ).astype(BF16)
    partial_copy = pltpu.make_async_copy(partial, partial_hbm, out_sem.at[3])
    partial_copy.start()
    attended_copy.wait()
    placing_copy.wait()
    marks_copy.wait()
    for copy in packed_copies:
        copy.wait()
    partial_copy.wait()


def attend(
    queries,
    fresh_k,
    fresh_v,
    cache_k,
    cache_v,
    weight,
    lengths,
    place,
    column,
    adapters,
    owners,
    resident,
    columns,
):
    requests, steps, width = queries.shape
    cache_size, kv_width = cache_k.shape[1:]
    capacity = max(2, 2 * requests // owners)
    block = min(32, requests)
    heads = width // HEAD_DIM
    total_rows = requests * steps
    per = capacity * steps
    anywhere = pl.BlockSpec(memory_space=pl.ANY)
    return pl.pallas_call(
        functools.partial(attend_kernel, owners, resident, capacity, block),
        grid_spec=pltpu.PrefetchScalarGridSpec(
            num_scalar_prefetch=3,
            grid=(1,),
            in_specs=[pl.BlockSpec((1, requests), lambda i, *_: (0, 0))] + [anywhere] * 6,
            out_specs=[anywhere] * (4 + owners),
            scratch_shapes=[
                pltpu.VMEM((requests, steps, width), BF16),
                pltpu.VMEM((requests, steps, kv_width), BF16),
                pltpu.VMEM((requests, steps, kv_width), BF16),
                pltpu.VMEM((requests, cache_size, kv_width), BF16),
                pltpu.VMEM((requests, cache_size, kv_width), BF16),
                pltpu.VMEM((width, columns), BF16),
                pltpu.VMEM((total_rows, kv_width), BF16),
                pltpu.VMEM((total_rows, kv_width), BF16),
                pltpu.VMEM((heads * block * steps, HEAD_DIM), F32),
                pltpu.VMEM((heads * total_rows, HEAD_DIM), F32),
                pltpu.VMEM((total_rows, width), BF16),
                pltpu.VMEM((owners * per, total_rows), BF16),
                pltpu.VMEM((total_rows, LANES), BF16),
                pltpu.VMEM((total_rows, columns), BF16),
                pltpu.VMEM((owners * per, width + LANES), BF16),
                pltpu.SemaphoreType.DMA((3,)),
                pltpu.SemaphoreType.DMA((2, requests // block)),
                pltpu.SemaphoreType.DMA((1,)),
                pltpu.SemaphoreType.DMA((4 + owners,)),
            ],
        ),
        out_shape=[
            jax.ShapeDtypeStruct((total_rows, width), BF16),
            jax.ShapeDtypeStruct((owners * per, total_rows), BF16),
            jax.ShapeDtypeStruct((total_rows, LANES), BF16),
            jax.ShapeDtypeStruct((total_rows, columns), BF16),
        ]
        + [jax.ShapeDtypeStruct((per, width + LANES), BF16)] * owners,
        compiler_params=pltpu.CompilerParams(vmem_limit_bytes=KERNEL_VMEM),
        cost_estimate=SMALL_COST,
        name="attend",
    )(
        lengths,
        place,
        column,
        adapters.reshape(1, requests),
        queries,
        fresh_k,
        fresh_v,
        cache_k,
        cache_v,
        weight,
    )


def project_kernel(count, *refs):
    places = refs[:count]
    attended_hbm, weight_hbm = refs[count : count + 2]
    outs = refs[count + 2 : 2 * count + 2]
    attended, weight, results, in_sem, weight_sem, out_sem = refs[2 * count + 2 :]
    columns = results.shape[2]
    attended_copy = pltpu.make_async_copy(attended_hbm, attended, in_sem.at[0])
    attended_copy.start()
    copies = []
    for j in range(count):
        start = pl.multiple_of(places[j][0] * columns, LANES)
        copy = pltpu.make_async_copy(
            weight_hbm.at[:, pl.ds(start, columns)], weight.at[j], weight_sem.at[j]
        )
        copy.start()
        copies.append(copy)
    attended_copy.wait()
    tile = min(256, columns)
    writes = []
    for j in range(count):
        copies[j].wait()
        for c in range(0, columns, tile):
            results[j, :, c : c + tile] = contract(
                attended[...], weight[j, :, c : c + tile], 1, 0
            ).astype(BF16)
        write = pltpu.make_async_copy(results.at[j], outs[j], out_sem.at[j])
        write.start()
        writes.append(write)
    for write in writes:
        write.wait()


def project(attended, weight, places, blocks):
    rows, depth = attended.shape
    columns = weight.shape[1] // blocks
    count = len(places)
    anywhere = pl.BlockSpec(memory_space=pl.ANY)
    return pl.pallas_call(
        functools.partial(project_kernel, count),
        grid_spec=pltpu.PrefetchScalarGridSpec(
            num_scalar_prefetch=count,
            grid=(1,),
            in_specs=[anywhere] * 2,
            out_specs=[anywhere] * count,
            scratch_shapes=[
                pltpu.VMEM((rows, depth), BF16),
                pltpu.VMEM((count, depth, columns), BF16),
                pltpu.VMEM((count, rows, columns), BF16),
                pltpu.SemaphoreType.DMA((1,)),
                pltpu.SemaphoreType.DMA((count,)),
                pltpu.SemaphoreType.DMA((count,)),
            ],
        ),
        out_shape=[jax.ShapeDtypeStruct((rows, columns), BF16)] * count,
        compiler_params=pltpu.CompilerParams(vmem_limit_bytes=KERNEL_VMEM),
        cost_estimate=SMALL_COST,
        name="project",
    )(*places, attended, weight)


def low_kernel(owners, resident, down, *refs):
    packed = refs[:owners]
    outs = refs[owners:]
    depth = down.shape[1]
    rank = down.shape[0] // resident
    weight = down[...]
    for k in range(owners):
        every = contract(packed[k][:, :depth], weight, 1, 1)
        marks = packed[k][:, depth:].astype(F32)
        low = every[:, :rank] * marks[:, 0:1]
        for y in range(1, resident):
            low = low + every[:, y * rank : (y + 1) * rank] * marks[:, y : y + 1]
        outs[k][...] = jnp.concatenate([low, jnp.zeros_like(low)], axis=1).astype(BF16)


def low_partial(packed, down):
    resident, rank, depth = down.shape
    owners = len(packed)
    per = packed[0].shape[0]
    return pl.pallas_call(
        functools.partial(low_kernel, owners, resident),
        out_shape=[jax.ShapeDtypeStruct((per, 2 * rank), BF16)] * owners,
        compiler_params=pltpu.CompilerParams(vmem_limit_bytes=SMALL_VMEM),
        cost_estimate=SMALL_COST,
        name="low",
    )(down.reshape(resident * rank, depth), *packed)


def unpack_kernel(placing, *refs):
    out = refs[-1]
    slots = jnp.concatenate([part[...] for part in refs[:-1]], axis=0)
    low = contract(placing[...], slots, 0, 0)
    half = low.shape[0] // 2
    rank = low.shape[1] // 2
    out[...] = jnp.concatenate([low[:half, :rank], low[half:, :rank]], axis=1).astype(BF16)


def unpack(placing, slots):
    rows = placing.shape[1]
    return pl.pallas_call(
        unpack_kernel,
        out_shape=jax.ShapeDtypeStruct((rows // 2, slots[0].shape[1]), BF16),
        compiler_params=pltpu.CompilerParams(vmem_limit_bytes=SMALL_VMEM),
        cost_estimate=SMALL_COST,
        name="unpack",
    )(placing, *slots)


def combine_kernel(blocks, resident, marks, *refs):
    partials = refs[:blocks]
    lows = refs[blocks : 2 * blocks]
    ups = refs[2 * blocks : -1]
    out = refs[-1]
    base = partials[0][...].astype(F32)
    low = lows[0][...].astype(F32)
    for part in partials[1:]:
        base = base + part[...].astype(F32)
    for part in lows[1:]:
        low = low + part[...].astype(F32)
    rank = low.shape[1] // 2
    low = low.astype(BF16).astype(F32)
    low = jnp.concatenate([low[:, :rank], low[:, rank:]], axis=0)
    chosen = marks[...].astype(F32)
    first = 0
    for up in ups:
        held = up.shape[0] // rank
        spread = jnp.concatenate(
            [low * chosen[:, y : y + 1] for y in range(first, first + held)], axis=1
        ).astype(BF16)
        base = base + contract(spread, up[...], 1, 0)
        first += held
    out[...] = base.reshape(out.shape).astype(BF16)


def combine(marks, partials, lows, ups, resident, steps):
    rows, columns = partials[0].shape
    return pl.pallas_call(
        functools.partial(combine_kernel, len(partials), resident),
        out_shape=jax.ShapeDtypeStruct((rows // steps, steps, columns), BF16),
        compiler_params=pltpu.CompilerParams(vmem_limit_bytes=SMALL_VMEM),
        cost_estimate=SMALL_COST,
        name="combine",
    )(marks, *partials, *lows, *ups)


def swap(value, axis, k):
    count = lax.axis_size(axis)
    return lax.ppermute(value, axis, [(i, i ^ k) for i in range(count)])


def forward(held, axis, bit):
    while bit:
        for k in list(held):
            if k ^ bit not in held:
                held[k ^ bit] = swap(held[k], axis, bit)
        bit //= 2


def body(
    queries,
    token_key_rows,
    token_value_rows,
    cached_key_rows,
    cached_value_rows,
    cache_length,
    request_adapter,
    output_weight_matrix,
    adapter_down_weight,
    adapter_up_weight,
):
    requests, steps, _ = queries.shape
    owners = lax.axis_size("adapter")
    blocks = lax.axis_size("tensor")
    resident, rank, columns = adapter_up_weight.shape
    place = lax.axis_index("adapter").reshape(1)
    mine = lax.axis_index("tensor")
    columns_of = lambda k: jnp.bitwise_xor(mine, k).reshape(1)

    up_rows = adapter_up_weight.reshape(resident * rank, columns)
    top_bit = owners // 2
    ups = {0: up_rows}
    ups[top_bit] = swap(up_rows, "adapter", top_bit)
    ups[1] = swap(up_rows, "adapter", 1)

    far = blocks - 1
    attended, placing, marks, first_partial, *packed = attend(
        queries,
        token_key_rows,
        token_value_rows,
        cached_key_rows,
        cached_value_rows,
        output_weight_matrix,
        cache_length,
        place,
        columns_of(far),
        request_adapter,
        owners,
        resident,
        columns,
    )
    ups[1], attended, first_partial, packed = lax.optimization_barrier(
        (ups[1], attended, first_partial, packed)
    )
    arrived = [packed[0]] + [None] * (owners - 1)
    for k in range(owners - 1, 0, -1):
        arrived[k] = swap(packed[k], "adapter", k)
    partials = {far: swap(first_partial, "tensor", far)}
    others = list(range(far - 1, 0, -1))
    made = project(attended, output_weight_matrix, [columns_of(k) for k in others], blocks)
    made, arrived[1], ups[top_bit] = lax.optimization_barrier(
        (made, arrived[1], ups[top_bit])
    )
    for k, part in zip(others, made):
        partials[k] = swap(part, "tensor", k)
    (own,) = project(attended, output_weight_matrix, [mine.reshape(1)], blocks)
    arrived, partials[far], own = lax.optimization_barrier((arrived, partials[far], own))
    lows = low_partial(arrived, adapter_down_weight)
    returned = [lows[0]] + [swap(lows[k], "adapter", k) for k in range(1, owners)]
    returned, partials = lax.optimization_barrier((returned, partials))
    low = unpack(placing, returned)
    ups, low = lax.optimization_barrier((ups, low))
    low_parts = [low] + [swap(low, "tensor", k) for k in range(1, blocks)]
    forward(ups, "adapter", top_bit // 2)
    return combine(
        marks,
        [own] + [partials[k] for k in range(1, blocks)],
        low_parts,
        [ups[k] for k in range(owners)],
        resident,
        steps,
    )


def solution(mesh):
    rows = P(("group", "adapter"), None, "tensor")
    return jax.shard_map(
        body,
        mesh=mesh,
        in_specs=(
            rows,
            rows,
            rows,
            rows,
            rows,
            P(("group", "adapter")),
            P(("group", "adapter")),
            P("tensor", None),
            rows,
            rows,
        ),
        out_specs=rows,
        check_vma=False,
    )
```

```python
import functools
import math

import jax
import jax.numpy as jnp
from jax import lax
from jax.experimental import pallas as pl
from jax.experimental.pallas import tpu as pltpu
from jax.sharding import PartitionSpec as P

HEAD_DIM = 128
NEGATIVE = -1e30
LANES = 128
KERNEL_VMEM = 56 * 1024 * 1024
SMALL_COST = pl.CostEstimate(flops=1024, bytes_accessed=1024, transcendentals=0)
SMALL_VMEM = 12 * 1024 * 1024

F32 = jnp.float32
BF16 = jnp.bfloat16


def contract(a, b, a_dim, b_dim):
    return lax.dot_general(
        a, b, (((a_dim,), (b_dim,)), ((), ())), preferred_element_type=F32
    )


def attend_kernel(
    owners,
    blocks,
    resident,
    capacity,
    block,
    lengths,
    place,
    column,
    adapters,
    queries_hbm,
    fresh_k_hbm,
    fresh_v_hbm,
    cache_k_hbm,
    cache_v_hbm,
    weight_hbm,
    *rest,
):
    placing_out, marks_out = rest[:2]
    partials = rest[2 : 2 + blocks]
    packed = rest[2 + blocks : 2 + blocks + owners]
    (
        queries,
        fresh_k,
        fresh_v,
        cache_k,
        cache_v,
        weight,
        new_k,
        new_v,
        query_scratch,
        result_scratch,
        attended,
        small_sem,
        cache_sem,
        weight_sem,
    ) = rest[2 + blocks + owners :]
    requests, steps, width = queries.shape
    heads = width // HEAD_DIM
    groups = cache_k.shape[2] // HEAD_DIM
    sharing = heads // groups
    cache_size = cache_k.shape[1]
    rows = block * steps
    total_rows = requests * steps
    span = steps * sharing
    chunks = requests // block
    columns = weight.shape[2]

    def cache_copies(i):
        part = pl.ds(i * block, block)
        return (
            pltpu.make_async_copy(cache_k_hbm.at[part], cache_k.at[part], cache_sem.at[0, i]),
            pltpu.make_async_copy(cache_v_hbm.at[part], cache_v.at[part], cache_sem.at[1, i]),
        )

    small = [
        pltpu.make_async_copy(queries_hbm, queries, small_sem.at[0]),
        pltpu.make_async_copy(fresh_k_hbm, fresh_k, small_sem.at[1]),
        pltpu.make_async_copy(fresh_v_hbm, fresh_v, small_sem.at[2]),
    ]
    for copy in small:
        copy.start()
    for i in range(chunks):
        for copy in cache_copies(i):
            copy.start()
    weight_copies = []
    for k in range(blocks - 1, -1, -1):
        start = pl.multiple_of(jnp.bitwise_xor(column[0], k) * columns, LANES)
        copy = pltpu.make_async_copy(
            weight_hbm.at[:, pl.ds(start, columns)], weight.at[k], weight_sem.at[k]
        )
        copy.start()
        weight_copies.append((k, copy))

    named = adapters[...]
    owner = lax.div(named, resident)
    local = named - owner * resident
    relative = jnp.bitwise_xor(owner, place[0])
    owner_id = lax.broadcasted_iota(jnp.int32, (owners, requests), 0)
    member = (owner_id == relative).astype(F32)
    before = lax.broadcasted_iota(jnp.int32, (requests, requests), 0) < (
        lax.broadcasted_iota(jnp.int32, (requests, requests), 1)
    )
    earlier = contract(member.astype(BF16), before.astype(BF16), 1, 0)
    slot = jnp.sum(earlier * member, axis=0, keepdims=True)
    facts = jnp.concatenate(
        [relative.astype(F32), slot, local.astype(F32), jnp.zeros((5, requests), F32)], axis=0
    )
    spread = lax.broadcasted_iota(jnp.int32, (requests, total_rows), 0) == lax.div(
        lax.broadcasted_iota(jnp.int32, (requests, total_rows), 1), steps
    )
    facts = contract(facts.astype(BF16), spread.astype(BF16), 1, 0).astype(jnp.int32)
    token = lax.rem(lax.broadcasted_iota(jnp.int32, (1, total_rows), 1), steps)
    target = (facts[0:1] * capacity + facts[1:2]) * steps + token
    slots = owners * capacity * steps
    placing = (
        lax.broadcasted_iota(jnp.int32, (slots, total_rows), 0) == target
    ).astype(BF16)
    placing_out[...] = placing
    chosen = (
        lax.broadcasted_iota(jnp.int32, (LANES, total_rows), 0) == facts[2:3]
    ).astype(BF16)
    per = capacity * steps
    carried = contract(placing, chosen, 1, 1).astype(BF16)
    for k in range(owners):
        packed[k][:, width:] = carried[k * per : (k + 1) * per]
    adapter_id = lax.broadcasted_iota(jnp.int32, (LANES, total_rows), 0)
    named_here = (adapter_id == facts[0:1] * resident + facts[2:3]).astype(BF16)
    identity = lax.broadcasted_iota(jnp.int32, (total_rows, total_rows), 0) == (
        lax.broadcasted_iota(jnp.int32, (total_rows, total_rows), 1)
    )
    marks_out[...] = contract(identity.astype(BF16), named_here, 1, 1).astype(BF16)

    positions = lax.broadcasted_iota(jnp.int32, (groups * span, cache_size), 1)
    row_id = lax.broadcasted_iota(jnp.int32, (block * groups * span, total_rows), 0)
    col_id = lax.broadcasted_iota(jnp.int32, (block * groups * span, total_rows), 1)
    distance = lax.div(row_id, groups * span) - lax.div(col_id, steps)
    causal = lax.rem(col_id, steps) <= lax.div(lax.rem(row_id, span), sharing)
    distance = jnp.where(causal, distance, requests)
    scaling = math.log2(math.e) / math.sqrt(HEAD_DIM)
    for copy in small:
        copy.wait()
    new_k[...] = fresh_k[...].reshape(total_rows, groups * HEAD_DIM)
    new_v[...] = fresh_v[...].reshape(total_rows, groups * HEAD_DIM)

    @pl.loop(0, chunks)
    def _(i):
        base = i * block
        flat = queries[pl.ds(base, block)].astype(F32).reshape(rows, width)
        for h in range(heads):
            query_scratch[h * rows : (h + 1) * rows, :] = flat[
                :, h * HEAD_DIM : (h + 1) * HEAD_DIM
            ]
        for copy in cache_copies(i):
            copy.wait()
        live_fresh = distance == -base
        empty = jnp.zeros((span, HEAD_DIM), BF16)
        wide = []
        for r in range(block):
            for g in range(groups):
                parts = []
                for s in range(steps):
                    start = g * sharing * rows + r * steps + s
                    parts.append(query_scratch[pl.ds(start, sharing, stride=rows), :])
                q = jnp.concatenate(parts, axis=0).astype(BF16)
                wide.append(
                    jnp.concatenate([q if o == g else empty for o in range(groups)], axis=1)
                )
        q = jnp.concatenate(wide, axis=0)
        fresh = jnp.where(live_fresh, contract(q, new_k[...], 1, 1), NEGATIVE)
        band = groups * span
        cached = []
        for r in range(block):
            score = contract(q[r * band : (r + 1) * band], cache_k[base + r], 1, 1)
            cached.append(jnp.where(positions < lengths[base + r], score, NEGATIVE))
        cached = jnp.concatenate(cached, axis=0)
        top = jnp.max(jnp.maximum(cached, fresh), axis=1, keepdims=True)
        cached = jnp.exp2((cached - top) * scaling)
        fresh = jnp.exp2((fresh - top) * scaling)
        scale = 1.0 / jnp.sum(cached + fresh, axis=1, keepdims=True)
        cached = cached.astype(BF16)
        out = contract(fresh.astype(BF16), new_v[...], 1, 0)
        for r in range(block):
            rows_r = slice(r * band, (r + 1) * band)
            both = (
                contract(cached[rows_r], cache_v[base + r], 1, 0) + out[rows_r]
            )
            for g in range(groups):
                for s in range(steps):
                    first = g * span + s * sharing
                    piece = both[
                        first : first + sharing, g * HEAD_DIM : (g + 1) * HEAD_DIM
                    ] * scale[r * band + first : r * band + first + sharing]
                    start = g * sharing * total_rows + (base + r) * steps + s
                    result_scratch[pl.ds(start, sharing, stride=total_rows), :] = piece

    for h in range(heads):
        attended[:, h * HEAD_DIM : (h + 1) * HEAD_DIM] = result_scratch[
            h * total_rows : (h + 1) * total_rows, :
        ].astype(BF16)
    tile = min(512, width)
    for c in range(0, width, tile):
        moved = contract(placing_out[...], attended[:, c : c + tile], 1, 0).astype(BF16)
        for k in range(owners):
            packed[k][:, c : c + tile] = moved[k * per : (k + 1) * per]
    tile = min(256, columns)
    for k, copy in weight_copies:
        copy.wait()
        for c in range(0, columns, tile):
            partials[k][:, c : c + tile] = contract(
                attended[...], weight[k, :, c : c + tile], 1, 0
            ).astype(BF16)


def attend(
    queries,
    fresh_k,
    fresh_v,
    cache_k,
    cache_v,
    weight,
    lengths,
    place,
    column,
    adapters,
    owners,
    resident,
    blocks,
    columns,
):
    requests, steps, width = queries.shape
    cache_size, kv_width = cache_k.shape[1:]
    capacity = max(2, 2 * requests // owners)
    block = min(32, requests)
    heads = width // HEAD_DIM
    total_rows = requests * steps
    per = capacity * steps
    anywhere = pl.BlockSpec(memory_space=pl.ANY)
    local = pl.BlockSpec(memory_space=pltpu.VMEM)
    return pl.pallas_call(
        functools.partial(attend_kernel, owners, blocks, resident, capacity, block),
        grid_spec=pltpu.PrefetchScalarGridSpec(
            num_scalar_prefetch=3,
            in_specs=[local] + [anywhere] * 6,
            out_specs=[local] * (2 + blocks + owners),
            scratch_shapes=[
                pltpu.VMEM((requests, steps, width), BF16),
                pltpu.VMEM((requests, steps, kv_width), BF16),
                pltpu.VMEM((requests, steps, kv_width), BF16),
                pltpu.VMEM((requests, cache_size, kv_width), BF16),
                pltpu.VMEM((requests, cache_size, kv_width), BF16),
                pltpu.VMEM((blocks, width, columns), BF16),
                pltpu.VMEM((total_rows, kv_width), BF16),
                pltpu.VMEM((total_rows, kv_width), BF16),
                pltpu.VMEM((heads * block * steps, HEAD_DIM), F32),
                pltpu.VMEM((heads * total_rows, HEAD_DIM), F32),
                pltpu.VMEM((total_rows, width), BF16),
                pltpu.SemaphoreType.DMA((3,)),
                pltpu.SemaphoreType.DMA((2, requests // block)),
                pltpu.SemaphoreType.DMA((blocks,)),
            ],
        ),
        out_shape=[
            jax.ShapeDtypeStruct((owners * per, total_rows), BF16),
            jax.ShapeDtypeStruct((total_rows, LANES), BF16),
        ]
        + [jax.ShapeDtypeStruct((total_rows, columns), BF16)] * blocks
        + [jax.ShapeDtypeStruct((per, width + LANES), BF16)] * owners,
        compiler_params=pltpu.CompilerParams(vmem_limit_bytes=KERNEL_VMEM),
        cost_estimate=SMALL_COST,
        name="attend",
    )(
        lengths,
        place,
        column,
        adapters.reshape(1, requests),
        queries,
        fresh_k,
        fresh_v,
        cache_k,
        cache_v,
        weight,
    )


def low_kernel(owners, resident, down, *refs):
    packed = refs[:owners]
    outs = refs[owners:]
    depth = down.shape[1]
    rank = down.shape[0] // resident
    weight = down[...]
    for k in range(owners):
        every = contract(packed[k][:, :depth], weight, 1, 1)
        marks = packed[k][:, depth:].astype(F32)
        low = every[:, :rank] * marks[:, 0:1]
        for y in range(1, resident):
            low = low + every[:, y * rank : (y + 1) * rank] * marks[:, y : y + 1]
        outs[k][...] = jnp.concatenate([low, jnp.zeros_like(low)], axis=1).astype(BF16)


def low_partial(packed, down):
    resident, rank, depth = down.shape
    owners = len(packed)
    per = packed[0].shape[0]
    return pl.pallas_call(
        functools.partial(low_kernel, owners, resident),
        out_shape=[jax.ShapeDtypeStruct((per, 2 * rank), BF16)] * owners,
        compiler_params=pltpu.CompilerParams(vmem_limit_bytes=SMALL_VMEM),
        cost_estimate=SMALL_COST,
        name="low",
    )(down.reshape(resident * rank, depth), *packed)


def unpack_kernel(placing, *refs):
    out = refs[-1]
    slots = jnp.concatenate([part[...] for part in refs[:-1]], axis=0)
    low = contract(placing[...], slots, 0, 0)
    half = low.shape[0] // 2
    rank = low.shape[1] // 2
    out[...] = jnp.concatenate([low[:half, :rank], low[half:, :rank]], axis=1).astype(BF16)


def unpack(placing, slots):
    rows = placing.shape[1]
    return pl.pallas_call(
        unpack_kernel,
        out_shape=jax.ShapeDtypeStruct((rows // 2, slots[0].shape[1]), BF16),
        compiler_params=pltpu.CompilerParams(vmem_limit_bytes=SMALL_VMEM),
        cost_estimate=SMALL_COST,
        name="unpack",
    )(placing, *slots)


def combine_kernel(sums, pairs, blocks, marks, *refs):
    partials = refs[:sums]
    halves = refs[sums : sums + 2 * pairs]
    refs = refs[:sums] + refs[sums + 2 * pairs :]
    lows = refs[sums : sums + blocks]
    ups = refs[sums + blocks : -1]
    out = refs[-1]
    low = lows[0][...].astype(F32)
    for part in lows[1:]:
        low = low + part[...].astype(F32)
    rank = low.shape[1] // 2
    low = low.astype(BF16).astype(F32)
    low = jnp.concatenate([low[:, :rank], low[:, rank:]], axis=0)
    chosen = marks[...].astype(F32)
    base = partials[0][...].astype(F32)
    for part in partials[1:]:
        base = base + part[...].astype(F32)
    for j in range(pairs):
        both = jnp.concatenate([halves[2 * j][...], halves[2 * j + 1][...]], axis=0)
        base = base + both.astype(F32)
    first = 0
    for up in ups:
        held = up.shape[0] // rank
        spread = jnp.concatenate(
            [low * chosen[:, y : y + 1] for y in range(first, first + held)], axis=1
        ).astype(BF16)
        base = base + contract(spread, up[...], 1, 0)
        first += held
    out[...] = base.reshape(out.shape).astype(BF16)


def combine(marks, own, partials, halves, lows, ups, steps):
    rows, columns = own.shape
    split = [part for pair in halves for part in pair]
    inputs = [marks, own, *partials, *split, *lows, *ups]
    return pl.pallas_call(
        functools.partial(
            combine_kernel, 1 + len(partials), len(halves), len(lows)
        ),
        out_shape=jax.ShapeDtypeStruct((rows // steps, steps, columns), BF16),
        compiler_params=pltpu.CompilerParams(vmem_limit_bytes=SMALL_VMEM),
        cost_estimate=SMALL_COST,
        name="combine",
    )(*inputs)


def swap(value, axis, k):
    count = lax.axis_size(axis)
    return lax.ppermute(value, axis, [(i, i ^ k) for i in range(count)])


def forward(held, axis, bit):
    while bit:
        for k in list(held):
            if k ^ bit not in held:
                held[k ^ bit] = swap(held[k], axis, bit)
        bit //= 2


def body(
    queries,
    token_key_rows,
    token_value_rows,
    cached_key_rows,
    cached_value_rows,
    cache_length,
    request_adapter,
    output_weight_matrix,
    adapter_down_weight,
    adapter_up_weight,
):
    requests, steps, _ = queries.shape
    owners = lax.axis_size("adapter")
    blocks = lax.axis_size("tensor")
    resident, rank, columns = adapter_up_weight.shape
    place = lax.axis_index("adapter").reshape(1)
    mine = lax.axis_index("tensor").reshape(1)

    up_rows = adapter_up_weight.reshape(resident * rank, columns)
    top_bit = owners // 2
    ups = {0: up_rows}
    ups[top_bit] = swap(up_rows, "adapter", top_bit)
    ups[1] = swap(up_rows, "adapter", 1)

    placing, marks, *made = attend(
        queries,
        token_key_rows,
        token_value_rows,
        cached_key_rows,
        cached_value_rows,
        output_weight_matrix,
        cache_length,
        place,
        mine,
        request_adapter,
        owners,
        resident,
        blocks,
        columns,
    )
    ups[1], made = lax.optimization_barrier((ups[1], made))
    partials, packed = made[:blocks], made[blocks:]
    inward = {k: swap(partials[k], "tensor", 1) for k in range(blocks - 1, 1, -2)}
    arrived = [packed[0]] + [None] * (owners - 1)
    for k in range(owners - 1, 0, -1):
        arrived[k] = swap(packed[k], "adapter", k)
    partials, inward, arrived[1], ups[top_bit] = lax.optimization_barrier(
        (partials, inward, arrived[1], ups[top_bit])
    )
    near = swap(partials[1], "tensor", 1)
    half = requests * steps // 2
    top, bottom = [], []
    for k in range(2, blocks, 2):
        pair = partials[k].astype(F32) + inward[k + 1].astype(F32)
        pair = pair.astype(BF16)
        top.append(swap(pair[:half], "tensor", k))
        bottom.append(swap(pair[half:], "tensor", k))
    arrived, near, top = lax.optimization_barrier((arrived, near, top))
    forward(ups, "adapter", top_bit // 2)
    lows = low_partial(arrived, adapter_down_weight)

    returned = [lows[0]] + [swap(lows[k], "adapter", k) for k in range(1, owners)]
    returned, bottom = lax.optimization_barrier((returned, bottom))
    low = unpack(placing, returned)
    low_parts = [low] + [swap(low, "tensor", k) for k in range(1, blocks)]
    return combine(
        marks,
        partials[0],
        [near],
        [*zip(top, bottom)],
        low_parts,
        [ups[k] for k in range(owners)],
        steps,
    )


def solution(mesh):
    rows = P(("group", "adapter"), None, "tensor")
    return jax.shard_map(
        body,
        mesh=mesh,
        in_specs=(
            rows,
            rows,
            rows,
            rows,
            rows,
            P(("group", "adapter")),
            P(("group", "adapter")),
            P("tensor", None),
            rows,
            rows,
        ),
        out_specs=rows,
        check_vma=False,
    )
```

```python
import functools
import math

import jax
import jax.numpy as jnp
from jax import lax
from jax.experimental import pallas as pl
from jax.experimental.pallas import tpu as pltpu
from jax.sharding import PartitionSpec as P

HEAD_DIM = 128
AHEAD = 4
NEGATIVE = -1e30
LANES = 128
KERNEL_VMEM = 56 * 1024 * 1024
SMALL_COST = pl.CostEstimate(flops=1024, bytes_accessed=1024, transcendentals=0)
SMALL_VMEM = 12 * 1024 * 1024

F32 = jnp.float32
BF16 = jnp.bfloat16


def contract(a, b, a_dim, b_dim):
    return lax.dot_general(
        a, b, (((a_dim,), (b_dim,)), ((), ())), preferred_element_type=F32
    )


def attend_kernel(
    owners,
    made,
    resident,
    capacity,
    block,
    lengths,
    place,
    column,
    adapters,
    queries_hbm,
    fresh_k_hbm,
    fresh_v_hbm,
    cache_k_hbm,
    cache_v_hbm,
    weight_hbm,
    *rest,
):
    attended, placing_out, marks_out, partial = rest[:4]
    packed = rest[4 : 4 + owners]
    (
        queries,
        fresh_k,
        fresh_v,
        cache_k,
        cache_v,
        weight,
        new_k,
        new_v,
        query_scratch,
        result_scratch,
        small_sem,
        cache_sem,
        weight_sem,
    ) = rest[4 + owners :]
    requests, steps, width = queries.shape
    heads = width // HEAD_DIM
    groups = cache_k.shape[2] // HEAD_DIM
    sharing = heads // groups
    cache_size = cache_k.shape[1]
    rows = block * steps
    total_rows = requests * steps
    span = steps * sharing
    chunks = requests // block
    columns = weight.shape[1]

    def cache_copies(i):
        part = pl.ds(i * block, block)
        return (
            pltpu.make_async_copy(cache_k_hbm.at[part], cache_k.at[part], cache_sem.at[0, i]),
            pltpu.make_async_copy(cache_v_hbm.at[part], cache_v.at[part], cache_sem.at[1, i]),
        )

    small = [
        pltpu.make_async_copy(queries_hbm, queries, small_sem.at[0]),
        pltpu.make_async_copy(fresh_k_hbm, fresh_k, small_sem.at[1]),
        pltpu.make_async_copy(fresh_v_hbm, fresh_v, small_sem.at[2]),
    ]
    start = pl.multiple_of(jnp.bitwise_xor(column[0], made) * columns, LANES)
    weight_copy = pltpu.make_async_copy(
        weight_hbm.at[:, pl.ds(start, columns)], weight, weight_sem.at[0]
    )
    for copy in (*small, *cache_copies(0)):
        copy.start()

    named = adapters[...]
    owner = lax.div(named, resident)
    local = named - owner * resident
    relative = jnp.bitwise_xor(owner, place[0])
    owner_id = lax.broadcasted_iota(jnp.int32, (owners, requests), 0)
    member = (owner_id == relative).astype(F32)
    before = lax.broadcasted_iota(jnp.int32, (requests, requests), 0) < (
        lax.broadcasted_iota(jnp.int32, (requests, requests), 1)
    )
    earlier = contract(member.astype(BF16), before.astype(BF16), 1, 0)
    slot = jnp.sum(earlier * member, axis=0, keepdims=True)
    facts = jnp.concatenate(
        [relative.astype(F32), slot, local.astype(F32), jnp.zeros((5, requests), F32)], axis=0
    )
    spread = lax.broadcasted_iota(jnp.int32, (requests, total_rows), 0) == lax.div(
        lax.broadcasted_iota(jnp.int32, (requests, total_rows), 1), steps
    )
    facts = contract(facts.astype(BF16), spread.astype(BF16), 1, 0).astype(jnp.int32)
    token = lax.rem(lax.broadcasted_iota(jnp.int32, (1, total_rows), 1), steps)
    target = (facts[0:1] * capacity + facts[1:2]) * steps + token
    slots = owners * capacity * steps
    placing = (
        lax.broadcasted_iota(jnp.int32, (slots, total_rows), 0) == target
    ).astype(BF16)
    placing_out[...] = placing
    chosen = (
        lax.broadcasted_iota(jnp.int32, (LANES, total_rows), 0) == facts[2:3]
    ).astype(BF16)
    per = capacity * steps
    carried = contract(placing, chosen, 1, 1).astype(BF16)
    for k in range(owners):
        packed[k][:, width:] = carried[k * per : (k + 1) * per]
    adapter_id = lax.broadcasted_iota(jnp.int32, (LANES, total_rows), 0)
    named_here = (adapter_id == facts[0:1] * resident + facts[2:3]).astype(BF16)
    identity = lax.broadcasted_iota(jnp.int32, (total_rows, total_rows), 0) == (
        lax.broadcasted_iota(jnp.int32, (total_rows, total_rows), 1)
    )
    marks_out[...] = contract(identity.astype(BF16), named_here, 1, 1).astype(BF16)

    positions = lax.broadcasted_iota(jnp.int32, (groups * span, cache_size), 1)
    row_id = lax.broadcasted_iota(jnp.int32, (block * groups * span, total_rows), 0)
    col_id = lax.broadcasted_iota(jnp.int32, (block * groups * span, total_rows), 1)
    distance = lax.div(row_id, groups * span) - lax.div(col_id, steps)
    causal = lax.rem(col_id, steps) <= lax.div(lax.rem(row_id, span), sharing)
    distance = jnp.where(causal, distance, requests)
    scaling = math.log2(math.e) / math.sqrt(HEAD_DIM)
    for copy in small:
        copy.wait()
    for i in range(1, min(AHEAD, chunks)):
        for copy in cache_copies(i):
            copy.start()
    new_k[...] = fresh_k[...].reshape(total_rows, groups * HEAD_DIM)
    new_v[...] = fresh_v[...].reshape(total_rows, groups * HEAD_DIM)

    @pl.loop(0, chunks)
    def _(i):
        base = i * block
        flat = queries[pl.ds(base, block)].astype(F32).reshape(rows, width)
        for h in range(heads):
            query_scratch[h * rows : (h + 1) * rows, :] = flat[
                :, h * HEAD_DIM : (h + 1) * HEAD_DIM
            ]
        for copy in cache_copies(i):
            copy.wait()

        @pl.when(i + AHEAD < chunks)
        def _():
            for copy in cache_copies(i + AHEAD):
                copy.start()

        @pl.when(i == min(1, chunks - 1))
        def _():
            weight_copy.start()

        live_fresh = distance == -base
        empty = jnp.zeros((span, HEAD_DIM), BF16)
        wide = []
        for r in range(block):
            for g in range(groups):
                parts = []
                for s in range(steps):
                    start = g * sharing * rows + r * steps + s
                    parts.append(query_scratch[pl.ds(start, sharing, stride=rows), :])
                q = jnp.concatenate(parts, axis=0).astype(BF16)
                wide.append(
                    jnp.concatenate([q if o == g else empty for o in range(groups)], axis=1)
                )
        q = jnp.concatenate(wide, axis=0)
        fresh = jnp.where(live_fresh, contract(q, new_k[...], 1, 1), NEGATIVE)
        band = groups * span
        cached = []
        for r in range(block):
            score = contract(q[r * band : (r + 1) * band], cache_k[base + r], 1, 1)
            cached.append(jnp.where(positions < lengths[base + r], score, NEGATIVE))
        cached = jnp.concatenate(cached, axis=0)
        top = jnp.max(jnp.maximum(cached, fresh), axis=1, keepdims=True)
        cached = jnp.exp2((cached - top) * scaling)
        fresh = jnp.exp2((fresh - top) * scaling)
        scale = 1.0 / jnp.sum(cached + fresh, axis=1, keepdims=True)
        cached = cached.astype(BF16)
        out = contract(fresh.astype(BF16), new_v[...], 1, 0)
        for r in range(block):
            rows_r = slice(r * band, (r + 1) * band)
            both = (
                contract(cached[rows_r], cache_v[base + r], 1, 0) + out[rows_r]
            )
            for g in range(groups):
                for s in range(steps):
                    first = g * span + s * sharing
                    piece = both[
                        first : first + sharing, g * HEAD_DIM : (g + 1) * HEAD_DIM
                    ] * scale[r * band + first : r * band + first + sharing]
                    start = g * sharing * total_rows + (base + r) * steps + s
                    result_scratch[pl.ds(start, sharing, stride=total_rows), :] = piece

    for h in range(heads):
        attended[:, h * HEAD_DIM : (h + 1) * HEAD_DIM] = result_scratch[
            h * total_rows : (h + 1) * total_rows, :
        ].astype(BF16)
    tile = min(512, width)
    for c in range(0, width, tile):
        moved = contract(placing_out[...], attended[:, c : c + tile], 1, 0).astype(BF16)
        for k in range(owners):
            packed[k][:, c : c + tile] = moved[k * per : (k + 1) * per]
    weight_copy.wait()
    tile = min(256, columns)
    for c in range(0, columns, tile):
        partial[:, c : c + tile] = contract(
            attended[...], weight[:, c : c + tile], 1, 0
        ).astype(BF16)


def attend(
    queries,
    fresh_k,
    fresh_v,
    cache_k,
    cache_v,
    weight,
    lengths,
    place,
    column,
    adapters,
    owners,
    resident,
    blocks,
    columns,
):
    requests, steps, width = queries.shape
    cache_size, kv_width = cache_k.shape[1:]
    capacity = max(2, 2 * requests // owners)
    block = min(16, requests)
    heads = width // HEAD_DIM
    total_rows = requests * steps
    per = capacity * steps
    anywhere = pl.BlockSpec(memory_space=pl.ANY)
    local = pl.BlockSpec(memory_space=pltpu.VMEM)
    return pl.pallas_call(
        functools.partial(attend_kernel, owners, blocks - 1, resident, capacity, block),
        grid_spec=pltpu.PrefetchScalarGridSpec(
            num_scalar_prefetch=3,
            in_specs=[local] + [anywhere] * 6,
            out_specs=[local] * (4 + owners),
            scratch_shapes=[
                pltpu.VMEM((requests, steps, width), BF16),
                pltpu.VMEM((requests, steps, kv_width), BF16),
                pltpu.VMEM((requests, steps, kv_width), BF16),
                pltpu.VMEM((requests, cache_size, kv_width), BF16),
                pltpu.VMEM((requests, cache_size, kv_width), BF16),
                pltpu.VMEM((width, columns), BF16),
                pltpu.VMEM((total_rows, kv_width), BF16),
                pltpu.VMEM((total_rows, kv_width), BF16),
                pltpu.VMEM((heads * block * steps, HEAD_DIM), F32),
                pltpu.VMEM((heads * total_rows, HEAD_DIM), F32),
                pltpu.SemaphoreType.DMA((3,)),
                pltpu.SemaphoreType.DMA((2, requests // block)),
                pltpu.SemaphoreType.DMA((1,)),
            ],
        ),
        out_shape=[
            jax.ShapeDtypeStruct((total_rows, width), BF16),
            jax.ShapeDtypeStruct((owners * per, total_rows), BF16),
            jax.ShapeDtypeStruct((total_rows, LANES), BF16),
            jax.ShapeDtypeStruct((total_rows, columns), BF16),
        ]
        + [jax.ShapeDtypeStruct((per, width + LANES), BF16)] * owners,
        compiler_params=pltpu.CompilerParams(vmem_limit_bytes=KERNEL_VMEM),
        cost_estimate=SMALL_COST,
        name="attend",
    )(
        lengths,
        place,
        column,
        adapters.reshape(1, requests),
        queries,
        fresh_k,
        fresh_v,
        cache_k,
        cache_v,
        weight,
    )


def project_kernel(count, *refs):
    column = refs[0]
    refs = refs[1:]
    attended_hbm, weight_hbm = refs[:2]
    outs = refs[2 : 2 + count]
    attended, weight, in_sem, weight_sem = refs[2 + count :]
    columns = weight.shape[2]
    attended_copy = pltpu.make_async_copy(attended_hbm, attended, in_sem.at[0])
    attended_copy.start()
    copies = []
    for j in range(count):
        start = pl.multiple_of(jnp.bitwise_xor(column[0], count - 1 - j) * columns, LANES)
        copy = pltpu.make_async_copy(
            weight_hbm.at[:, pl.ds(start, columns)], weight.at[j], weight_sem.at[j]
        )
        copy.start()
        copies.append(copy)
    attended_copy.wait()
    tile = min(256, columns)
    for j in range(count):
        copies[j].wait()
        for c in range(0, columns, tile):
            outs[j][:, c : c + tile] = contract(
                attended[...], weight[j, :, c : c + tile], 1, 0
            ).astype(BF16)


def project(attended, weight, column, blocks):
    rows, depth = attended.shape
    columns = weight.shape[1] // blocks
    count = blocks - 1
    local = pl.BlockSpec(memory_space=pltpu.VMEM)
    anywhere = pl.BlockSpec(memory_space=pl.ANY)
    return pl.pallas_call(
        functools.partial(project_kernel, count),
        grid_spec=pltpu.PrefetchScalarGridSpec(
            num_scalar_prefetch=1,
            in_specs=[anywhere] * 2,
            out_specs=[local] * count,
            scratch_shapes=[
                pltpu.VMEM((rows, depth), BF16),
                pltpu.VMEM((count, depth, columns), BF16),
                pltpu.SemaphoreType.DMA((1,)),
                pltpu.SemaphoreType.DMA((count,)),
            ],
        ),
        out_shape=[jax.ShapeDtypeStruct((rows, columns), BF16)] * count,
        compiler_params=pltpu.CompilerParams(vmem_limit_bytes=KERNEL_VMEM),
        cost_estimate=SMALL_COST,
        name="project",
    )(column, attended, weight)


def low_kernel(owners, resident, down, *refs):
    packed = refs[:owners]
    outs = refs[owners:]
    depth = down.shape[1]
    rank = down.shape[0] // resident
    weight = down[...]
    for k in range(owners):
        every = contract(packed[k][:, :depth], weight, 1, 1)
        marks = packed[k][:, depth:].astype(F32)
        low = every[:, :rank] * marks[:, 0:1]
        for y in range(1, resident):
            low = low + every[:, y * rank : (y + 1) * rank] * marks[:, y : y + 1]
        outs[k][...] = jnp.concatenate([low, jnp.zeros_like(low)], axis=1).astype(BF16)


def low_partial(packed, down):
    resident, rank, depth = down.shape
    owners = len(packed)
    per = packed[0].shape[0]
    return pl.pallas_call(
        functools.partial(low_kernel, owners, resident),
        out_shape=[jax.ShapeDtypeStruct((per, 2 * rank), BF16)] * owners,
        compiler_params=pltpu.CompilerParams(vmem_limit_bytes=SMALL_VMEM),
        cost_estimate=SMALL_COST,
        name="low",
    )(down.reshape(resident * rank, depth), *packed)


def unpack_kernel(placing, *refs):
    out = refs[-1]
    slots = jnp.concatenate([part[...] for part in refs[:-1]], axis=0)
    low = contract(placing[...], slots, 0, 0)
    half = low.shape[0] // 2
    rank = low.shape[1] // 2
    out[...] = jnp.concatenate([low[:half, :rank], low[half:, :rank]], axis=1).astype(BF16)


def unpack(placing, slots):
    rows = placing.shape[1]
    return pl.pallas_call(
        unpack_kernel,
        out_shape=jax.ShapeDtypeStruct((rows // 2, slots[0].shape[1]), BF16),
        compiler_params=pltpu.CompilerParams(vmem_limit_bytes=SMALL_VMEM),
        cost_estimate=SMALL_COST,
        name="unpack",
    )(placing, *slots)


def combine_kernel(sums, pairs, blocks, marks, *refs):
    partials = refs[:sums]
    halves = refs[sums : sums + 2 * pairs]
    refs = refs[:sums] + refs[sums + 2 * pairs :]
    lows = refs[sums : sums + blocks]
    ups = refs[sums + blocks : -1]
    out = refs[-1]
    low = lows[0][...].astype(F32)
    for part in lows[1:]:
        low = low + part[...].astype(F32)
    rank = low.shape[1] // 2
    low = low.astype(BF16).astype(F32)
    low = jnp.concatenate([low[:, :rank], low[:, rank:]], axis=0)
    chosen = marks[...].astype(F32)
    base = partials[0][...].astype(F32)
    for part in partials[1:]:
        base = base + part[...].astype(F32)
    for j in range(pairs):
        both = jnp.concatenate([halves[2 * j][...], halves[2 * j + 1][...]], axis=0)
        base = base + both.astype(F32)
    first = 0
    for up in ups:
        held = up.shape[0] // rank
        spread = jnp.concatenate(
            [low * chosen[:, y : y + 1] for y in range(first, first + held)], axis=1
        ).astype(BF16)
        base = base + contract(spread, up[...], 1, 0)
        first += held
    out[...] = base.reshape(out.shape).astype(BF16)


def combine(marks, own, partials, halves, lows, ups, steps):
    rows, columns = own.shape
    split = [part for pair in halves for part in pair]
    inputs = [marks, own, *partials, *split, *lows, *ups]
    return pl.pallas_call(
        functools.partial(
            combine_kernel, 1 + len(partials), len(halves), len(lows)
        ),
        out_shape=jax.ShapeDtypeStruct((rows // steps, steps, columns), BF16),
        compiler_params=pltpu.CompilerParams(vmem_limit_bytes=SMALL_VMEM),
        cost_estimate=SMALL_COST,
        name="combine",
    )(*inputs)


def swap(value, axis, k):
    count = lax.axis_size(axis)
    return lax.ppermute(value, axis, [(i, i ^ k) for i in range(count)])


def forward(held, axis, bit):
    while bit:
        for k in list(held):
            if k ^ bit not in held:
                held[k ^ bit] = swap(held[k], axis, bit)
        bit //= 2


def body(
    queries,
    token_key_rows,
    token_value_rows,
    cached_key_rows,
    cached_value_rows,
    cache_length,
    request_adapter,
    output_weight_matrix,
    adapter_down_weight,
    adapter_up_weight,
):
    requests, steps, _ = queries.shape
    owners = lax.axis_size("adapter")
    blocks = lax.axis_size("tensor")
    resident, rank, columns = adapter_up_weight.shape
    place = lax.axis_index("adapter").reshape(1)
    mine = lax.axis_index("tensor").reshape(1)

    up_rows = adapter_up_weight.reshape(resident * rank, columns)
    top_bit = owners // 2
    ups = {0: up_rows}
    ups[top_bit] = swap(up_rows, "adapter", top_bit)
    ups[1] = swap(up_rows, "adapter", 1)

    attended, placing, marks, first, *packed = attend(
        queries,
        token_key_rows,
        token_value_rows,
        cached_key_rows,
        cached_value_rows,
        output_weight_matrix,
        cache_length,
        place,
        mine,
        request_adapter,
        owners,
        resident,
        blocks,
        columns,
    )
    ups[1], attended, first, packed = lax.optimization_barrier(
        (ups[1], attended, first, packed)
    )
    inward = {blocks - 1: swap(first, "tensor", 1)}
    arrived = [packed[0]] + [None] * (owners - 1)
    for k in range(owners - 1, 0, -1):
        arrived[k] = swap(packed[k], "adapter", k)
    made = project(attended, output_weight_matrix, mine, blocks)
    partials = {blocks - 2 - j: part for j, part in enumerate(made)}
    for k in range(blocks - 3, 1, -2):
        inward[k] = swap(partials[k], "tensor", 1)
    partials, inward, arrived[1], ups[top_bit] = lax.optimization_barrier(
        (partials, inward, arrived[1], ups[top_bit])
    )
    outward = []
    for k in range(2, blocks, 2):
        pair = partials[k].astype(F32) + inward[k + 1].astype(F32)
        outward.append(swap(pair.astype(BF16), "tensor", k))
    near = swap(partials[1], "tensor", 1)
    arrived, near, outward = lax.optimization_barrier((arrived, near, outward))
    lows = low_partial(arrived, adapter_down_weight)
    ups, lows = lax.optimization_barrier((ups, lows))
    forward(ups, "adapter", top_bit // 2)
    returned = [lows[0]] + [swap(lows[k], "adapter", k) for k in range(1, owners)]

    low = unpack(placing, returned)
    low_parts = [low] + [swap(low, "tensor", k) for k in range(1, blocks)]
    return combine(
        marks,
        partials[0],
        [near] + outward,
        [],
        low_parts,
        [ups[k] for k in range(owners)],
        steps,
    )


def solution(mesh):
    rows = P(("group", "adapter"), None, "tensor")
    return jax.shard_map(
        body,
        mesh=mesh,
        in_specs=(
            rows,
            rows,
            rows,
            rows,
            rows,
            P(("group", "adapter")),
            P(("group", "adapter")),
            P("tensor", None),
            rows,
            rows,
        ),
        out_specs=rows,
        check_vma=False,
    )
```

```python
import functools
import math

import jax
import jax.numpy as jnp
from jax import lax
from jax.experimental import pallas as pl
from jax.experimental.pallas import tpu as pltpu
from jax.sharding import PartitionSpec as P

HEAD_DIM = 128
AHEAD = 4
NEGATIVE = -1e30
LANES = 128
KERNEL_VMEM = 56 * 1024 * 1024
SMALL_COST = pl.CostEstimate(flops=1024, bytes_accessed=1024, transcendentals=0)
SMALL_VMEM = 16 * 1024 * 1024

F32 = jnp.float32
BF16 = jnp.bfloat16


def contract(a, b, a_dim, b_dim):
    return lax.dot_general(
        a, b, (((a_dim,), (b_dim,)), ((), ())), preferred_element_type=F32
    )


def attend_kernel(
    made,
    resident,
    block,
    lengths,
    place,
    column,
    adapters,
    queries_hbm,
    fresh_k_hbm,
    fresh_v_hbm,
    cache_k_hbm,
    cache_v_hbm,
    weight_hbm,
    *rest,
):
    attended, marks_out, partial = rest[:3]
    (
        queries,
        fresh_k,
        fresh_v,
        cache_k,
        cache_v,
        weight,
        new_k,
        new_v,
        query_scratch,
        result_scratch,
        small_sem,
        cache_sem,
        weight_sem,
    ) = rest[3:]
    requests, steps, width = queries.shape
    heads = width // HEAD_DIM
    groups = cache_k.shape[2] // HEAD_DIM
    sharing = heads // groups
    cache_size = cache_k.shape[1]
    rows = block * steps
    total_rows = requests * steps
    span = steps * sharing
    chunks = requests // block
    columns = weight.shape[1]

    def cache_copies(i):
        part = pl.ds(i * block, block)
        return (
            pltpu.make_async_copy(cache_k_hbm.at[part], cache_k.at[part], cache_sem.at[0, i]),
            pltpu.make_async_copy(cache_v_hbm.at[part], cache_v.at[part], cache_sem.at[1, i]),
        )

    small = [
        pltpu.make_async_copy(queries_hbm, queries, small_sem.at[0]),
        pltpu.make_async_copy(fresh_k_hbm, fresh_k, small_sem.at[1]),
        pltpu.make_async_copy(fresh_v_hbm, fresh_v, small_sem.at[2]),
    ]
    start = pl.multiple_of(jnp.bitwise_xor(column[0], made) * columns, LANES)
    weight_copy = pltpu.make_async_copy(
        weight_hbm.at[:, pl.ds(start, columns)], weight, weight_sem.at[0]
    )
    for copy in (*small, *cache_copies(0)):
        copy.start()

    named = adapters[...]
    owner = lax.div(named, resident)
    local = named - owner * resident
    relative = jnp.bitwise_xor(owner, place[0]) * resident + local
    facts = jnp.concatenate(
        [relative.astype(F32), jnp.zeros((7, requests), F32)], axis=0
    ).astype(BF16)
    spread = lax.broadcasted_iota(jnp.int32, (requests, total_rows), 0) == lax.div(
        lax.broadcasted_iota(jnp.int32, (requests, total_rows), 1), steps
    )
    facts = contract(facts, spread.astype(BF16), 1, 0).astype(jnp.int32)
    named_here = (
        lax.broadcasted_iota(jnp.int32, (LANES, total_rows), 0) == facts[0:1]
    ).astype(BF16)
    identity = lax.broadcasted_iota(jnp.int32, (total_rows, total_rows), 0) == (
        lax.broadcasted_iota(jnp.int32, (total_rows, total_rows), 1)
    )
    marks_out[...] = contract(identity.astype(BF16), named_here, 1, 1).astype(BF16)

    positions = lax.broadcasted_iota(jnp.int32, (groups * span, cache_size), 1)
    row_id = lax.broadcasted_iota(jnp.int32, (block * groups * span, total_rows), 0)
    col_id = lax.broadcasted_iota(jnp.int32, (block * groups * span, total_rows), 1)
    distance = lax.div(row_id, groups * span) - lax.div(col_id, steps)
    causal = lax.rem(col_id, steps) <= lax.div(lax.rem(row_id, span), sharing)
    distance = jnp.where(causal, distance, requests)
    scaling = math.log2(math.e) / math.sqrt(HEAD_DIM)
    for copy in small:
        copy.wait()
    for i in range(1, min(AHEAD, chunks)):
        for copy in cache_copies(i):
            copy.start()
    new_k[...] = fresh_k[...].reshape(total_rows, groups * HEAD_DIM)
    new_v[...] = fresh_v[...].reshape(total_rows, groups * HEAD_DIM)

    @pl.loop(0, chunks)
    def _(i):
        base = i * block
        flat = queries[pl.ds(base, block)].astype(F32).reshape(rows, width)
        for h in range(heads):
            query_scratch[h * rows : (h + 1) * rows, :] = flat[
                :, h * HEAD_DIM : (h + 1) * HEAD_DIM
            ]
        for copy in cache_copies(i):
            copy.wait()

        @pl.when(i + AHEAD < chunks)
        def _():
            for copy in cache_copies(i + AHEAD):
                copy.start()

        @pl.when(i == min(1, chunks - 1))
        def _():
            weight_copy.start()

        live_fresh = distance == -base
        empty = jnp.zeros((span, HEAD_DIM), BF16)
        wide = []
        for r in range(block):
            for g in range(groups):
                parts = []
                for s in range(steps):
                    start = g * sharing * rows + r * steps + s
                    parts.append(query_scratch[pl.ds(start, sharing, stride=rows), :])
                q = jnp.concatenate(parts, axis=0).astype(BF16)
                wide.append(
                    jnp.concatenate([q if o == g else empty for o in range(groups)], axis=1)
                )
        q = jnp.concatenate(wide, axis=0)
        fresh = jnp.where(live_fresh, contract(q, new_k[...], 1, 1), NEGATIVE)
        band = groups * span
        cached = []
        for r in range(block):
            score = contract(q[r * band : (r + 1) * band], cache_k[base + r], 1, 1)
            cached.append(jnp.where(positions < lengths[base + r], score, NEGATIVE))
        cached = jnp.concatenate(cached, axis=0)
        top = jnp.max(jnp.maximum(cached, fresh), axis=1, keepdims=True)
        cached = jnp.exp2((cached - top) * scaling)
        fresh = jnp.exp2((fresh - top) * scaling)
        scale = 1.0 / jnp.sum(cached + fresh, axis=1, keepdims=True)
        cached = cached.astype(BF16)
        out = contract(fresh.astype(BF16), new_v[...], 1, 0)
        for r in range(block):
            rows_r = slice(r * band, (r + 1) * band)
            both = (
                contract(cached[rows_r], cache_v[base + r], 1, 0) + out[rows_r]
            )
            for g in range(groups):
                for s in range(steps):
                    first = g * span + s * sharing
                    piece = both[
                        first : first + sharing, g * HEAD_DIM : (g + 1) * HEAD_DIM
                    ] * scale[r * band + first : r * band + first + sharing]
                    start = g * sharing * total_rows + (base + r) * steps + s
                    result_scratch[pl.ds(start, sharing, stride=total_rows), :] = piece

    for h in range(heads):
        attended[:, h * HEAD_DIM : (h + 1) * HEAD_DIM] = result_scratch[
            h * total_rows : (h + 1) * total_rows, :
        ].astype(BF16)
    weight_copy.wait()
    tile = min(256, columns)
    for c in range(0, columns, tile):
        partial[:, c : c + tile] = contract(
            attended[...], weight[:, c : c + tile], 1, 0
        ).astype(BF16)


def attend(
    queries,
    fresh_k,
    fresh_v,
    cache_k,
    cache_v,
    weight,
    lengths,
    place,
    column,
    adapters,
    resident,
    blocks,
    columns,
):
    requests, steps, width = queries.shape
    cache_size, kv_width = cache_k.shape[1:]
    block = min(16, requests)
    heads = width // HEAD_DIM
    total_rows = requests * steps
    anywhere = pl.BlockSpec(memory_space=pl.ANY)
    local = pl.BlockSpec(memory_space=pltpu.VMEM)
    return pl.pallas_call(
        functools.partial(attend_kernel, blocks - 1, resident, block),
        grid_spec=pltpu.PrefetchScalarGridSpec(
            num_scalar_prefetch=3,
            in_specs=[local] + [anywhere] * 6,
            out_specs=[local] * 3,
            scratch_shapes=[
                pltpu.VMEM((requests, steps, width), BF16),
                pltpu.VMEM((requests, steps, kv_width), BF16),
                pltpu.VMEM((requests, steps, kv_width), BF16),
                pltpu.VMEM((requests, cache_size, kv_width), BF16),
                pltpu.VMEM((requests, cache_size, kv_width), BF16),
                pltpu.VMEM((width, columns), BF16),
                pltpu.VMEM((total_rows, kv_width), BF16),
                pltpu.VMEM((total_rows, kv_width), BF16),
                pltpu.VMEM((heads * block * steps, HEAD_DIM), F32),
                pltpu.VMEM((heads * total_rows, HEAD_DIM), F32),
                pltpu.SemaphoreType.DMA((3,)),
                pltpu.SemaphoreType.DMA((2, requests // block)),
                pltpu.SemaphoreType.DMA((1,)),
            ],
        ),
        out_shape=[
            jax.ShapeDtypeStruct((total_rows, width), BF16),
            jax.ShapeDtypeStruct((total_rows, LANES), BF16),
            jax.ShapeDtypeStruct((total_rows, columns), BF16),
        ],
        compiler_params=pltpu.CompilerParams(vmem_limit_bytes=KERNEL_VMEM),
        cost_estimate=SMALL_COST,
        name="attend",
    )(
        lengths,
        place,
        column,
        adapters.reshape(1, requests),
        queries,
        fresh_k,
        fresh_v,
        cache_k,
        cache_v,
        weight,
    )


def project_kernel(count, *refs):
    column = refs[0]
    refs = refs[1:]
    attended_hbm, weight_hbm = refs[:2]
    outs = refs[2 : 2 + count]
    attended, weight, in_sem, weight_sem = refs[2 + count :]
    columns = weight.shape[2]
    attended_copy = pltpu.make_async_copy(attended_hbm, attended, in_sem.at[0])
    attended_copy.start()
    copies = []
    for j in range(count):
        start = pl.multiple_of(jnp.bitwise_xor(column[0], count - 1 - j) * columns, LANES)
        copy = pltpu.make_async_copy(
            weight_hbm.at[:, pl.ds(start, columns)], weight.at[j], weight_sem.at[j]
        )
        copy.start()
        copies.append(copy)
    attended_copy.wait()
    tile = min(256, columns)
    for j in range(count):
        copies[j].wait()
        for c in range(0, columns, tile):
            outs[j][:, c : c + tile] = contract(
                attended[...], weight[j, :, c : c + tile], 1, 0
            ).astype(BF16)


def project(attended, weight, column, blocks):
    rows, depth = attended.shape
    columns = weight.shape[1] // blocks
    count = blocks - 1
    local = pl.BlockSpec(memory_space=pltpu.VMEM)
    anywhere = pl.BlockSpec(memory_space=pl.ANY)
    return pl.pallas_call(
        functools.partial(project_kernel, count),
        grid_spec=pltpu.PrefetchScalarGridSpec(
            num_scalar_prefetch=1,
            in_specs=[anywhere] * 2,
            out_specs=[local] * count,
            scratch_shapes=[
                pltpu.VMEM((rows, depth), BF16),
                pltpu.VMEM((count, depth, columns), BF16),
                pltpu.SemaphoreType.DMA((1,)),
                pltpu.SemaphoreType.DMA((count,)),
            ],
        ),
        out_shape=[jax.ShapeDtypeStruct((rows, columns), BF16)] * count,
        compiler_params=pltpu.CompilerParams(vmem_limit_bytes=KERNEL_VMEM),
        cost_estimate=SMALL_COST,
        name="project",
    )(column, attended, weight)


def low_kernel(rank, attended, marks, *refs):
    out = refs[-1]
    rows = attended[...]
    chosen = marks[...].astype(F32)
    low = jnp.zeros((rows.shape[0], rank), F32)
    first = 0
    for down in refs[:-1]:
        every = contract(rows, down[...], 1, 1)
        for y in range(down.shape[0] // rank):
            part = every[:, y * rank : (y + 1) * rank]
            low = low + part * chosen[:, first : first + 1]
            first += 1
    half = low.shape[0] // 2
    out[...] = jnp.concatenate([low[:half], low[half:]], axis=1).astype(BF16)


def low_partial(attended, marks, downs, rank):
    rows = attended.shape[0]
    return pl.pallas_call(
        functools.partial(low_kernel, rank),
        out_shape=jax.ShapeDtypeStruct((rows // 2, 2 * rank), BF16),
        compiler_params=pltpu.CompilerParams(vmem_limit_bytes=SMALL_VMEM),
        cost_estimate=SMALL_COST,
        name="low",
    )(attended, marks, *downs)


def combine_kernel(sums, blocks, marks, *refs):
    partials = refs[:sums]
    lows = refs[sums : sums + blocks]
    ups = refs[sums + blocks : -1]
    out = refs[-1]
    low = lows[0][...].astype(F32)
    for part in lows[1:]:
        low = low + part[...].astype(F32)
    rank = low.shape[1] // 2
    low = low.astype(BF16).astype(F32)
    low = jnp.concatenate([low[:, :rank], low[:, rank:]], axis=0)
    chosen = marks[...].astype(F32)
    base = partials[0][...].astype(F32)
    for part in partials[1:]:
        base = base + part[...].astype(F32)
    first = 0
    for up in ups:
        held = up.shape[0] // rank
        spread = jnp.concatenate(
            [low * chosen[:, y : y + 1] for y in range(first, first + held)], axis=1
        ).astype(BF16)
        base = base + contract(spread, up[...], 1, 0)
        first += held
    out[...] = base.reshape(out.shape).astype(BF16)


def combine(marks, own, partials, lows, ups, steps):
    rows, columns = own.shape
    inputs = [marks, own, *partials, *lows, *ups]
    return pl.pallas_call(
        functools.partial(combine_kernel, 1 + len(partials), len(lows)),
        out_shape=jax.ShapeDtypeStruct((rows // steps, steps, columns), BF16),
        compiler_params=pltpu.CompilerParams(vmem_limit_bytes=SMALL_VMEM),
        cost_estimate=SMALL_COST,
        name="combine",
    )(*inputs)


def swap(value, axis, k):
    count = lax.axis_size(axis)
    return lax.ppermute(value, axis, [(i, i ^ k) for i in range(count)])


def forward(held, axis, bit):
    while bit:
        for k in list(held):
            if k ^ bit not in held:
                held[k ^ bit] = swap(held[k], axis, bit)
        bit //= 2


def body(
    queries,
    token_key_rows,
    token_value_rows,
    cached_key_rows,
    cached_value_rows,
    cache_length,
    request_adapter,
    output_weight_matrix,
    adapter_down_weight,
    adapter_up_weight,
):
    requests, steps, _ = queries.shape
    owners = lax.axis_size("adapter")
    blocks = lax.axis_size("tensor")
    resident, rank, columns = adapter_up_weight.shape
    place = lax.axis_index("adapter").reshape(1)
    mine = lax.axis_index("tensor").reshape(1)

    top_bit = owners // 2
    ups = {0: adapter_up_weight.reshape(resident * rank, columns)}
    downs = {0: adapter_down_weight.reshape(resident * rank, -1)}
    downs[top_bit] = swap(downs[0], "adapter", top_bit)
    cut = resident * rank // 2
    far_ups = [{top_bit: swap(ups[0][:cut], "adapter", top_bit)}]
    for held in (downs, ups):
        held[1] = swap(held[0], "adapter", 1)

    attended, marks, first = attend(
        queries,
        token_key_rows,
        token_value_rows,
        cached_key_rows,
        cached_value_rows,
        output_weight_matrix,
        cache_length,
        place,
        mine,
        request_adapter,
        resident,
        blocks,
        columns,
    )
    ups[1], downs[1], attended, first = lax.optimization_barrier(
        (ups[1], downs[1], attended, first)
    )
    inward = {blocks - 1: swap(first, "tensor", 1)}
    made = project(attended, output_weight_matrix, mine, blocks)
    partials = {blocks - 2 - j: part for j, part in enumerate(made)}
    for k in range(blocks - 3, 1, -2):
        inward[k] = swap(partials[k], "tensor", 1)
    partials, inward = lax.optimization_barrier((partials, inward))
    outward = []
    for k in range(2, blocks, 2):
        pair = partials[k].astype(F32) + inward[k + 1].astype(F32)
        outward.append(swap(pair.astype(BF16), "tensor", k))
    near = swap(partials[1], "tensor", 1)
    near = near.astype(F32) + partials[0].astype(F32)
    downs[top_bit], far_ups[0], near, outward = lax.optimization_barrier(
        (downs[top_bit], far_ups[0], near, outward)
    )
    forward(downs, "adapter", top_bit // 2)
    last_ups = ups[0][cut:]
    last_ups, near = lax.optimization_barrier((last_ups, near))
    far_ups.append({top_bit: swap(last_ups, "adapter", top_bit)})
    low = low_partial(attended, marks, [downs[k] for k in range(owners)], rank)
    low_parts = [low] + [swap(low, "tensor", k) for k in range(1, blocks)]
    far_ups[1], low_parts = lax.optimization_barrier((far_ups[1], low_parts))
    forward(ups, "adapter", top_bit // 2)
    for held in far_ups:
        forward(held, "adapter", top_bit // 2)
    pieces = []
    for k in range(owners):
        pieces += [ups[k]] if k < top_bit else [held[k] for held in far_ups]
    return combine(marks, near, outward, low_parts, pieces, steps)


def solution(mesh):
    rows = P(("group", "adapter"), None, "tensor")
    return jax.shard_map(
        body,
        mesh=mesh,
        in_specs=(
            rows,
            rows,
            rows,
            rows,
            rows,
            P(("group", "adapter")),
            P(("group", "adapter")),
            P("tensor", None),
            rows,
            rows,
        ),
        out_specs=rows,
        check_vma=False,
    )
```

```python
import functools
import math

import jax
import jax.numpy as jnp
from jax import lax
from jax.experimental import pallas as pl
from jax.experimental.pallas import tpu as pltpu
from jax.sharding import PartitionSpec as P

HEAD_DIM = 128
AHEAD = 4
NEGATIVE = -1e30
LANES = 128
KERNEL_VMEM = 56 * 1024 * 1024
SMALL_COST = pl.CostEstimate(flops=1024, bytes_accessed=1024, transcendentals=0)
SMALL_VMEM = 16 * 1024 * 1024

F32 = jnp.float32
BF16 = jnp.bfloat16


def contract(a, b, a_dim, b_dim):
    return lax.dot_general(
        a, b, (((a_dim,), (b_dim,)), ((), ())), preferred_element_type=F32
    )


def attend_kernel(
    made,
    resident,
    block,
    lengths,
    place,
    column,
    adapters,
    queries_hbm,
    fresh_k_hbm,
    fresh_v_hbm,
    cache_k_hbm,
    cache_v_hbm,
    weight_hbm,
    *rest,
):
    attended, marks_out, partial = rest[:3]
    (
        queries,
        fresh_k,
        fresh_v,
        cache_k,
        cache_v,
        weight,
        new_k,
        new_v,
        query_scratch,
        result_scratch,
        small_sem,
        cache_sem,
        weight_sem,
    ) = rest[3:]
    requests, steps, width = queries.shape
    heads = width // HEAD_DIM
    groups = cache_k.shape[2] // HEAD_DIM
    sharing = heads // groups
    cache_size = cache_k.shape[1]
    rows = block * steps
    total_rows = requests * steps
    span = steps * sharing
    chunks = requests // block
    columns = weight.shape[1]

    def cache_copies(i):
        part = pl.ds(i * block, block)
        return (
            pltpu.make_async_copy(cache_k_hbm.at[part], cache_k.at[part], cache_sem.at[0, i]),
            pltpu.make_async_copy(cache_v_hbm.at[part], cache_v.at[part], cache_sem.at[1, i]),
        )

    small = [
        pltpu.make_async_copy(queries_hbm, queries, small_sem.at[0]),
        pltpu.make_async_copy(fresh_k_hbm, fresh_k, small_sem.at[1]),
        pltpu.make_async_copy(fresh_v_hbm, fresh_v, small_sem.at[2]),
    ]
    start = pl.multiple_of(jnp.bitwise_xor(column[0], made) * columns, LANES)
    weight_copy = pltpu.make_async_copy(
        weight_hbm.at[:, pl.ds(start, columns)], weight, weight_sem.at[0]
    )
    for copy in (*small, *cache_copies(0)):
        copy.start()

    named = adapters[...]
    owner = lax.div(named, resident)
    local = named - owner * resident
    relative = jnp.bitwise_xor(owner, place[0]) * resident + local
    facts = jnp.concatenate(
        [relative.astype(F32), jnp.zeros((7, requests), F32)], axis=0
    ).astype(BF16)
    spread = lax.broadcasted_iota(jnp.int32, (requests, total_rows), 0) == lax.div(
        lax.broadcasted_iota(jnp.int32, (requests, total_rows), 1), steps
    )
    facts = contract(facts, spread.astype(BF16), 1, 0).astype(jnp.int32)
    named_here = (
        lax.broadcasted_iota(jnp.int32, (LANES, total_rows), 0) == facts[0:1]
    ).astype(BF16)
    identity = lax.broadcasted_iota(jnp.int32, (total_rows, total_rows), 0) == (
        lax.broadcasted_iota(jnp.int32, (total_rows, total_rows), 1)
    )
    marks_out[...] = contract(identity.astype(BF16), named_here, 1, 1).astype(BF16)

    positions = lax.broadcasted_iota(jnp.int32, (groups * span, cache_size), 1)
    row_id = lax.broadcasted_iota(jnp.int32, (block * groups * span, total_rows), 0)
    col_id = lax.broadcasted_iota(jnp.int32, (block * groups * span, total_rows), 1)
    distance = lax.div(row_id, groups * span) - lax.div(col_id, steps)
    causal = lax.rem(col_id, steps) <= lax.div(lax.rem(row_id, span), sharing)
    distance = jnp.where(causal, distance, requests)
    scaling = math.log2(math.e) / math.sqrt(HEAD_DIM)
    for copy in small:
        copy.wait()
    for i in range(1, min(AHEAD, chunks)):
        for copy in cache_copies(i):
            copy.start()
    new_k[...] = fresh_k[...].reshape(total_rows, groups * HEAD_DIM)
    new_v[...] = fresh_v[...].reshape(total_rows, groups * HEAD_DIM)

    @pl.loop(0, chunks)
    def _(i):
        base = i * block
        flat = queries[pl.ds(base, block)].astype(F32).reshape(rows, width)
        for h in range(heads):
            query_scratch[h * rows : (h + 1) * rows, :] = flat[
                :, h * HEAD_DIM : (h + 1) * HEAD_DIM
            ]
        for copy in cache_copies(i):
            copy.wait()

        @pl.when(i + AHEAD < chunks)
        def _():
            for copy in cache_copies(i + AHEAD):
                copy.start()

        @pl.when(i == min(1, chunks - 1))
        def _():
            weight_copy.start()

        live_fresh = distance == -base
        empty = jnp.zeros((span, HEAD_DIM), BF16)
        wide = []
        for r in range(block):
            for g in range(groups):
                parts = []
                for s in range(steps):
                    start = g * sharing * rows + r * steps + s
                    parts.append(query_scratch[pl.ds(start, sharing, stride=rows), :])
                q = jnp.concatenate(parts, axis=0).astype(BF16)
                wide.append(
                    jnp.concatenate([q if o == g else empty for o in range(groups)], axis=1)
                )
        q = jnp.concatenate(wide, axis=0)
        fresh = jnp.where(live_fresh, contract(q, new_k[...], 1, 1), NEGATIVE)
        band = groups * span
        cached = []
        for r in range(block):
            score = contract(q[r * band : (r + 1) * band], cache_k[base + r], 1, 1)
            cached.append(jnp.where(positions < lengths[base + r], score, NEGATIVE))
        cached = jnp.concatenate(cached, axis=0)
        top = jnp.max(jnp.maximum(cached, fresh), axis=1, keepdims=True)
        cached = jnp.exp2((cached - top) * scaling)
        fresh = jnp.exp2((fresh - top) * scaling)
        scale = 1.0 / jnp.sum(cached + fresh, axis=1, keepdims=True)
        cached = cached.astype(BF16)
        out = contract(fresh.astype(BF16), new_v[...], 1, 0)
        for r in range(block):
            rows_r = slice(r * band, (r + 1) * band)
            both = (
                contract(cached[rows_r], cache_v[base + r], 1, 0) + out[rows_r]
            )
            for g in range(groups):
                for s in range(steps):
                    first = g * span + s * sharing
                    piece = both[
                        first : first + sharing, g * HEAD_DIM : (g + 1) * HEAD_DIM
                    ] * scale[r * band + first : r * band + first + sharing]
                    start = g * sharing * total_rows + (base + r) * steps + s
                    result_scratch[pl.ds(start, sharing, stride=total_rows), :] = piece

    for h in range(heads):
        attended[:, h * HEAD_DIM : (h + 1) * HEAD_DIM] = result_scratch[
            h * total_rows : (h + 1) * total_rows, :
        ].astype(BF16)
    weight_copy.wait()
    tile = min(256, columns)
    for c in range(0, columns, tile):
        partial[:, c : c + tile] = contract(
            attended[...], weight[:, c : c + tile], 1, 0
        ).astype(BF16)


def attend(
    queries,
    fresh_k,
    fresh_v,
    cache_k,
    cache_v,
    weight,
    lengths,
    place,
    column,
    adapters,
    resident,
    blocks,
    columns,
):
    requests, steps, width = queries.shape
    cache_size, kv_width = cache_k.shape[1:]
    block = min(16, requests)
    heads = width // HEAD_DIM
    total_rows = requests * steps
    anywhere = pl.BlockSpec(memory_space=pl.ANY)
    local = pl.BlockSpec(memory_space=pltpu.VMEM)
    return pl.pallas_call(
        functools.partial(attend_kernel, blocks - 1, resident, block),
        grid_spec=pltpu.PrefetchScalarGridSpec(
            num_scalar_prefetch=3,
            in_specs=[local] + [anywhere] * 6,
            out_specs=[local] * 3,
            scratch_shapes=[
                pltpu.VMEM((requests, steps, width), BF16),
                pltpu.VMEM((requests, steps, kv_width), BF16),
                pltpu.VMEM((requests, steps, kv_width), BF16),
                pltpu.VMEM((requests, cache_size, kv_width), BF16),
                pltpu.VMEM((requests, cache_size, kv_width), BF16),
                pltpu.VMEM((width, columns), BF16),
                pltpu.VMEM((total_rows, kv_width), BF16),
                pltpu.VMEM((total_rows, kv_width), BF16),
                pltpu.VMEM((heads * block * steps, HEAD_DIM), F32),
                pltpu.VMEM((heads * total_rows, HEAD_DIM), F32),
                pltpu.SemaphoreType.DMA((3,)),
                pltpu.SemaphoreType.DMA((2, requests // block)),
                pltpu.SemaphoreType.DMA((1,)),
            ],
        ),
        out_shape=[
            jax.ShapeDtypeStruct((total_rows, width), BF16),
            jax.ShapeDtypeStruct((total_rows, LANES), BF16),
            jax.ShapeDtypeStruct((total_rows, columns), BF16),
        ],
        compiler_params=pltpu.CompilerParams(vmem_limit_bytes=KERNEL_VMEM),
        cost_estimate=SMALL_COST,
        name="attend",
    )(
        lengths,
        place,
        column,
        adapters.reshape(1, requests),
        queries,
        fresh_k,
        fresh_v,
        cache_k,
        cache_v,
        weight,
    )


def project_kernel(count, *refs):
    column = refs[0]
    refs = refs[1:]
    attended_hbm, weight_hbm = refs[:2]
    outs = refs[2 : 2 + count]
    attended, weight, in_sem, weight_sem = refs[2 + count :]
    columns = weight.shape[2]
    attended_copy = pltpu.make_async_copy(attended_hbm, attended, in_sem.at[0])
    attended_copy.start()
    copies = []
    for j in range(count):
        start = pl.multiple_of(jnp.bitwise_xor(column[0], count - 1 - j) * columns, LANES)
        copy = pltpu.make_async_copy(
            weight_hbm.at[:, pl.ds(start, columns)], weight.at[j], weight_sem.at[j]
        )
        copy.start()
        copies.append(copy)
    attended_copy.wait()
    tile = min(256, columns)
    for j in range(count):
        copies[j].wait()
        for c in range(0, columns, tile):
            outs[j][:, c : c + tile] = contract(
                attended[...], weight[j, :, c : c + tile], 1, 0
            ).astype(BF16)


def project(attended, weight, column, blocks):
    rows, depth = attended.shape
    columns = weight.shape[1] // blocks
    count = blocks - 1
    local = pl.BlockSpec(memory_space=pltpu.VMEM)
    anywhere = pl.BlockSpec(memory_space=pl.ANY)
    return pl.pallas_call(
        functools.partial(project_kernel, count),
        grid_spec=pltpu.PrefetchScalarGridSpec(
            num_scalar_prefetch=1,
            in_specs=[anywhere] * 2,
            out_specs=[local] * count,
            scratch_shapes=[
                pltpu.VMEM((rows, depth), BF16),
                pltpu.VMEM((count, depth, columns), BF16),
                pltpu.SemaphoreType.DMA((1,)),
                pltpu.SemaphoreType.DMA((count,)),
            ],
        ),
        out_shape=[jax.ShapeDtypeStruct((rows, columns), BF16)] * count,
        compiler_params=pltpu.CompilerParams(vmem_limit_bytes=KERNEL_VMEM),
        cost_estimate=SMALL_COST,
        name="project",
    )(column, attended, weight)


def low_kernel(rank, attended, marks, *refs):
    out = refs[-1]
    rows = attended[...]
    chosen = marks[...].astype(F32)
    low = jnp.zeros((rows.shape[0], rank), F32)
    first = 0
    for down in refs[:-1]:
        every = contract(rows, down[...], 1, 1)
        for y in range(down.shape[0] // rank):
            part = every[:, y * rank : (y + 1) * rank]
            low = low + part * chosen[:, first : first + 1]
            first += 1
    half = low.shape[0] // 2
    out[...] = jnp.concatenate([low[:half], low[half:]], axis=1).astype(BF16)


def low_partial(attended, marks, downs, rank):
    rows = attended.shape[0]
    return pl.pallas_call(
        functools.partial(low_kernel, rank),
        out_shape=jax.ShapeDtypeStruct((rows // 2, 2 * rank), BF16),
        compiler_params=pltpu.CompilerParams(vmem_limit_bytes=SMALL_VMEM),
        cost_estimate=SMALL_COST,
        name="low",
    )(attended, marks, *downs)


def combine_kernel(sums, blocks, marks, *refs):
    partials = refs[:sums]
    lows = refs[sums : sums + blocks]
    ups = refs[sums + blocks : -1]
    out = refs[-1]
    low = lows[0][...].astype(F32)
    for part in lows[1:]:
        low = low + part[...].astype(F32)
    rank = low.shape[1] // 2
    low = low.astype(BF16).astype(F32)
    low = jnp.concatenate([low[:, :rank], low[:, rank:]], axis=0)
    chosen = marks[...].astype(F32)
    base = partials[0][...].astype(F32)
    for part in partials[1:]:
        base = base + part[...].astype(F32)
    first = 0
    for up in ups:
        held = up.shape[0] // rank
        spread = jnp.concatenate(
            [low * chosen[:, y : y + 1] for y in range(first, first + held)], axis=1
        ).astype(BF16)
        base = base + contract(spread, up[...], 1, 0)
        first += held
    out[...] = base.reshape(out.shape).astype(BF16)


def combine(marks, own, partials, lows, ups, steps):
    rows, columns = own.shape
    inputs = [marks, own, *partials, *lows, *ups]
    return pl.pallas_call(
        functools.partial(combine_kernel, 1 + len(partials), len(lows)),
        out_shape=jax.ShapeDtypeStruct((rows // steps, steps, columns), BF16),
        compiler_params=pltpu.CompilerParams(vmem_limit_bytes=SMALL_VMEM),
        cost_estimate=SMALL_COST,
        name="combine",
    )(*inputs)


def swap(value, axis, k):
    count = lax.axis_size(axis)
    return lax.ppermute(value, axis, [(i, i ^ k) for i in range(count)])


def forward(held, axis, bit):
    while bit:
        for k in list(held):
            if k ^ bit not in held:
                held[k ^ bit] = swap(held[k], axis, bit)
        bit //= 2


def body(
    queries,
    token_key_rows,
    token_value_rows,
    cached_key_rows,
    cached_value_rows,
    cache_length,
    request_adapter,
    output_weight_matrix,
    adapter_down_weight,
    adapter_up_weight,
):
    requests, steps, _ = queries.shape
    owners = lax.axis_size("adapter")
    blocks = lax.axis_size("tensor")
    resident, rank, columns = adapter_up_weight.shape
    place = lax.axis_index("adapter").reshape(1)
    mine = lax.axis_index("tensor").reshape(1)

    top_bit = owners // 2
    ups = {0: adapter_up_weight.reshape(resident * rank, columns)}
    downs = {0: adapter_down_weight.reshape(resident * rank, -1)}
    downs[top_bit] = swap(downs[0], "adapter", top_bit)
    cut = resident * rank // 2
    far_ups = [{top_bit: swap(ups[0][:cut], "adapter", top_bit)}]
    for held in (downs, ups):
        held[1] = swap(held[0], "adapter", 1)

    attended, marks, first = attend(
        queries,
        token_key_rows,
        token_value_rows,
        cached_key_rows,
        cached_value_rows,
        output_weight_matrix,
        cache_length,
        place,
        mine,
        request_adapter,
        resident,
        blocks,
        columns,
    )
    ups[1], downs[1], attended, first = lax.optimization_barrier(
        (ups[1], downs[1], attended, first)
    )
    inward = {blocks - 1: swap(first, "tensor", 1)}
    made = project(attended, output_weight_matrix, mine, blocks)
    partials = {blocks - 2 - j: part for j, part in enumerate(made)}
    for k in range(blocks - 3, 1, -2):
        inward[k] = swap(partials[k], "tensor", 1)
    partials, inward = lax.optimization_barrier((partials, inward))
    outward = []
    for k in range(2, blocks, 2):
        pair = partials[k].astype(F32) + inward[k + 1].astype(F32)
        outward.append(swap(pair.astype(BF16), "tensor", k))
    near = swap(partials[1], "tensor", 1)
    near = near.astype(F32) + partials[0].astype(F32)
    downs[top_bit], far_ups[0], inw = lax.optimization_barrier((downs[top_bit], far_ups[0], outward))
    outward = inw
    forward(downs, "adapter", top_bit // 2)
    last_ups, outward = lax.optimization_barrier((ups[0][cut:], outward))
    far_ups.append({top_bit: swap(last_ups, "adapter", top_bit)})
    low = low_partial(attended, marks, [downs[k] for k in range(owners)], rank)
    low_parts = [low] + [swap(low, "tensor", k) for k in range(1, blocks)]
    far_ups[1], low_parts = lax.optimization_barrier((far_ups[1], low_parts))
    forward(ups, "adapter", top_bit // 2)
    for held in far_ups:
        forward(held, "adapter", top_bit // 2)
    pieces = []
    for k in range(owners):
        pieces += [ups[k]] if k < top_bit else [held[k] for held in far_ups]
    return combine(marks, near, outward, low_parts, pieces, steps)


def solution(mesh):
    rows = P(("group", "adapter"), None, "tensor")
    return jax.shard_map(
        body,
        mesh=mesh,
        in_specs=(
            rows,
            rows,
            rows,
            rows,
            rows,
            P(("group", "adapter")),
            P(("group", "adapter")),
            P("tensor", None),
            rows,
            rows,
        ),
        out_specs=rows,
        check_vma=False,
    )
```

```python
import functools
import math

import jax
import jax.numpy as jnp
from jax import lax
from jax.experimental import pallas as pl
from jax.experimental.pallas import tpu as pltpu
from jax.sharding import PartitionSpec as P

HEAD_DIM = 128
AHEAD = 4
NEGATIVE = -1e30
LANES = 128
KERNEL_VMEM = 56 * 1024 * 1024
SMALL_COST = pl.CostEstimate(flops=1024, bytes_accessed=1024, transcendentals=0)
SMALL_VMEM = 16 * 1024 * 1024

F32 = jnp.float32
BF16 = jnp.bfloat16


def contract(a, b, a_dim, b_dim):
    return lax.dot_general(
        a, b, (((a_dim,), (b_dim,)), ((), ())), preferred_element_type=F32
    )


def attend_kernel(
    made,
    resident,
    block,
    lengths,
    place,
    column,
    adapters,
    queries_hbm,
    fresh_k_hbm,
    fresh_v_hbm,
    cache_k_hbm,
    cache_v_hbm,
    weight_hbm,
    *rest,
):
    attended, marks_out, partial = rest[:3]
    (
        queries,
        fresh_k,
        fresh_v,
        cache_k,
        cache_v,
        weight,
        new_k,
        new_v,
        query_scratch,
        result_scratch,
        small_sem,
        cache_sem,
        weight_sem,
    ) = rest[3:]
    requests, steps, width = queries.shape
    heads = width // HEAD_DIM
    groups = cache_k.shape[2] // HEAD_DIM
    sharing = heads // groups
    cache_size = cache_k.shape[1]
    rows = block * steps
    total_rows = requests * steps
    span = steps * sharing
    chunks = requests // block
    columns = weight.shape[1]

    def cache_copies(i):
        part = pl.ds(i * block, block)
        return (
            pltpu.make_async_copy(cache_k_hbm.at[part], cache_k.at[part], cache_sem.at[0, i]),
            pltpu.make_async_copy(cache_v_hbm.at[part], cache_v.at[part], cache_sem.at[1, i]),
        )

    small = [
        pltpu.make_async_copy(queries_hbm, queries, small_sem.at[0]),
        pltpu.make_async_copy(fresh_k_hbm, fresh_k, small_sem.at[1]),
        pltpu.make_async_copy(fresh_v_hbm, fresh_v, small_sem.at[2]),
    ]
    start = pl.multiple_of(jnp.bitwise_xor(column[0], made) * columns, LANES)
    weight_copy = pltpu.make_async_copy(
        weight_hbm.at[:, pl.ds(start, columns)], weight, weight_sem.at[0]
    )
    for copy in (*small, *cache_copies(0)):
        copy.start()

    named = adapters[...]
    owner = lax.div(named, resident)
    local = named - owner * resident
    relative = jnp.bitwise_xor(owner, place[0]) * resident + local
    facts = jnp.concatenate(
        [relative.astype(F32), jnp.zeros((7, requests), F32)], axis=0
    ).astype(BF16)
    spread = lax.broadcasted_iota(jnp.int32, (requests, total_rows), 0) == lax.div(
        lax.broadcasted_iota(jnp.int32, (requests, total_rows), 1), steps
    )
    facts = contract(facts, spread.astype(BF16), 1, 0).astype(jnp.int32)
    named_here = (
        lax.broadcasted_iota(jnp.int32, (LANES, total_rows), 0) == facts[0:1]
    ).astype(BF16)
    identity = lax.broadcasted_iota(jnp.int32, (total_rows, total_rows), 0) == (
        lax.broadcasted_iota(jnp.int32, (total_rows, total_rows), 1)
    )
    marks_out[...] = contract(identity.astype(BF16), named_here, 1, 1).astype(BF16)

    positions = lax.broadcasted_iota(jnp.int32, (groups * span, cache_size), 1)
    row_id = lax.broadcasted_iota(jnp.int32, (block * groups * span, total_rows), 0)
    col_id = lax.broadcasted_iota(jnp.int32, (block * groups * span, total_rows), 1)
    distance = lax.div(row_id, groups * span) - lax.div(col_id, steps)
    causal = lax.rem(col_id, steps) <= lax.div(lax.rem(row_id, span), sharing)
    distance = jnp.where(causal, distance, requests)
    scaling = math.log2(math.e) / math.sqrt(HEAD_DIM)
    for copy in small:
        copy.wait()
    for i in range(1, min(AHEAD, chunks)):
        for copy in cache_copies(i):
            copy.start()
    new_k[...] = fresh_k[...].reshape(total_rows, groups * HEAD_DIM)
    new_v[...] = fresh_v[...].reshape(total_rows, groups * HEAD_DIM)

    @pl.loop(0, chunks)
    def _(i):
        base = i * block
        flat = queries[pl.ds(base, block)].astype(F32).reshape(rows, width)
        for h in range(heads):
            query_scratch[h * rows : (h + 1) * rows, :] = flat[
                :, h * HEAD_DIM : (h + 1) * HEAD_DIM
            ]
        for copy in cache_copies(i):
            copy.wait()

        @pl.when(i + AHEAD < chunks)
        def _():
            for copy in cache_copies(i + AHEAD):
                copy.start()

        @pl.when(i == min(1, chunks - 1))
        def _():
            weight_copy.start()

        live_fresh = distance == -base
        empty = jnp.zeros((span, HEAD_DIM), BF16)
        wide = []
        for r in range(block):
            for g in range(groups):
                parts = []
                for s in range(steps):
                    start = g * sharing * rows + r * steps + s
                    parts.append(query_scratch[pl.ds(start, sharing, stride=rows), :])
                q = jnp.concatenate(parts, axis=0).astype(BF16)
                wide.append(
                    jnp.concatenate([q if o == g else empty for o in range(groups)], axis=1)
                )
        q = jnp.concatenate(wide, axis=0)
        fresh = jnp.where(live_fresh, contract(q, new_k[...], 1, 1), NEGATIVE)
        band = groups * span
        cached = []
        for r in range(block):
            score = contract(q[r * band : (r + 1) * band], cache_k[base + r], 1, 1)
            cached.append(jnp.where(positions < lengths[base + r], score, NEGATIVE))
        cached = jnp.concatenate(cached, axis=0)
        top = jnp.max(jnp.maximum(cached, fresh), axis=1, keepdims=True)
        cached = jnp.exp2((cached - top) * scaling)
        fresh = jnp.exp2((fresh - top) * scaling)
        scale = 1.0 / jnp.sum(cached + fresh, axis=1, keepdims=True)
        cached = cached.astype(BF16)
        out = contract(fresh.astype(BF16), new_v[...], 1, 0)
        for r in range(block):
            rows_r = slice(r * band, (r + 1) * band)
            both = (
                contract(cached[rows_r], cache_v[base + r], 1, 0) + out[rows_r]
            )
            for g in range(groups):
                for s in range(steps):
                    first = g * span + s * sharing
                    piece = both[
                        first : first + sharing, g * HEAD_DIM : (g + 1) * HEAD_DIM
                    ] * scale[r * band + first : r * band + first + sharing]
                    start = g * sharing * total_rows + (base + r) * steps + s
                    result_scratch[pl.ds(start, sharing, stride=total_rows), :] = piece

    for h in range(heads):
        attended[:, h * HEAD_DIM : (h + 1) * HEAD_DIM] = result_scratch[
            h * total_rows : (h + 1) * total_rows, :
        ].astype(BF16)
    weight_copy.wait()
    tile = min(256, columns)
    for c in range(0, columns, tile):
        partial[:, c : c + tile] = contract(
            attended[...], weight[:, c : c + tile], 1, 0
        ).astype(BF16)


def attend(
    queries,
    fresh_k,
    fresh_v,
    cache_k,
    cache_v,
    weight,
    lengths,
    place,
    column,
    adapters,
    resident,
    blocks,
    columns,
):
    requests, steps, width = queries.shape
    cache_size, kv_width = cache_k.shape[1:]
    block = min(16, requests)
    heads = width // HEAD_DIM
    total_rows = requests * steps
    anywhere = pl.BlockSpec(memory_space=pl.ANY)
    local = pl.BlockSpec(memory_space=pltpu.VMEM)
    return pl.pallas_call(
        functools.partial(attend_kernel, blocks - 1, resident, block),
        grid_spec=pltpu.PrefetchScalarGridSpec(
            num_scalar_prefetch=3,
            in_specs=[local] + [anywhere] * 6,
            out_specs=[local] * 3,
            scratch_shapes=[
                pltpu.VMEM((requests, steps, width), BF16),
                pltpu.VMEM((requests, steps, kv_width), BF16),
                pltpu.VMEM((requests, steps, kv_width), BF16),
                pltpu.VMEM((requests, cache_size, kv_width), BF16),
                pltpu.VMEM((requests, cache_size, kv_width), BF16),
                pltpu.VMEM((width, columns), BF16),
                pltpu.VMEM((total_rows, kv_width), BF16),
                pltpu.VMEM((total_rows, kv_width), BF16),
                pltpu.VMEM((heads * block * steps, HEAD_DIM), F32),
                pltpu.VMEM((heads * total_rows, HEAD_DIM), F32),
                pltpu.SemaphoreType.DMA((3,)),
                pltpu.SemaphoreType.DMA((2, requests // block)),
                pltpu.SemaphoreType.DMA((1,)),
            ],
        ),
        out_shape=[
            jax.ShapeDtypeStruct((total_rows, width), BF16),
            jax.ShapeDtypeStruct((total_rows, LANES), BF16),
            jax.ShapeDtypeStruct((total_rows, columns), BF16),
        ],
        compiler_params=pltpu.CompilerParams(vmem_limit_bytes=KERNEL_VMEM),
        cost_estimate=SMALL_COST,
        name="attend",
    )(
        lengths,
        place,
        column,
        adapters.reshape(1, requests),
        queries,
        fresh_k,
        fresh_v,
        cache_k,
        cache_v,
        weight,
    )


def project_kernel(count, *refs):
    column = refs[0]
    refs = refs[1:]
    attended_hbm, weight_hbm = refs[:2]
    outs = refs[2 : 2 + count]
    attended, weight, in_sem, weight_sem = refs[2 + count :]
    columns = weight.shape[2]
    attended_copy = pltpu.make_async_copy(attended_hbm, attended, in_sem.at[0])
    attended_copy.start()
    copies = []
    for j in range(count):
        start = pl.multiple_of(jnp.bitwise_xor(column[0], count - 1 - j) * columns, LANES)
        copy = pltpu.make_async_copy(
            weight_hbm.at[:, pl.ds(start, columns)], weight.at[j], weight_sem.at[j]
        )
        copy.start()
        copies.append(copy)
    attended_copy.wait()
    tile = min(256, columns)
    for j in range(count):
        copies[j].wait()
        for c in range(0, columns, tile):
            outs[j][:, c : c + tile] = contract(
                attended[...], weight[j, :, c : c + tile], 1, 0
            ).astype(BF16)


def project(attended, weight, column, blocks):
    rows, depth = attended.shape
    columns = weight.shape[1] // blocks
    count = blocks - 1
    local = pl.BlockSpec(memory_space=pltpu.VMEM)
    anywhere = pl.BlockSpec(memory_space=pl.ANY)
    return pl.pallas_call(
        functools.partial(project_kernel, count),
        grid_spec=pltpu.PrefetchScalarGridSpec(
            num_scalar_prefetch=1,
            in_specs=[anywhere] * 2,
            out_specs=[local] * count,
            scratch_shapes=[
                pltpu.VMEM((rows, depth), BF16),
                pltpu.VMEM((count, depth, columns), BF16),
                pltpu.SemaphoreType.DMA((1,)),
                pltpu.SemaphoreType.DMA((count,)),
            ],
        ),
        out_shape=[jax.ShapeDtypeStruct((rows, columns), BF16)] * count,
        compiler_params=pltpu.CompilerParams(vmem_limit_bytes=KERNEL_VMEM),
        cost_estimate=SMALL_COST,
        name="project",
    )(column, attended, weight)


def low_kernel(rank, attended, marks, *refs):
    out = refs[-1]
    rows = attended[...]
    chosen = marks[...].astype(F32)
    low = jnp.zeros((rows.shape[0], rank), F32)
    first = 0
    for down in refs[:-1]:
        every = contract(rows, down[...], 1, 1)
        for y in range(down.shape[0] // rank):
            part = every[:, y * rank : (y + 1) * rank]
            low = low + part * chosen[:, first : first + 1]
            first += 1
    half = low.shape[0] // 2
    out[...] = jnp.concatenate([low[:half], low[half:]], axis=1).astype(BF16)


def low_partial(attended, marks, downs, rank):
    rows = attended.shape[0]
    return pl.pallas_call(
        functools.partial(low_kernel, rank),
        out_shape=jax.ShapeDtypeStruct((rows // 2, 2 * rank), BF16),
        compiler_params=pltpu.CompilerParams(vmem_limit_bytes=SMALL_VMEM),
        cost_estimate=SMALL_COST,
        name="low",
    )(attended, marks, *downs)


def combine_kernel(pairs, blocks, marks, own, *refs):
    sums = 2 * pairs
    lows = refs[sums : sums + blocks]
    ups = refs[sums + blocks : -1]
    out = refs[-1]
    low = lows[0][...].astype(F32)
    for part in lows[1:]:
        low = low + part[...].astype(F32)
    rank = low.shape[1] // 2
    low = low.astype(BF16).astype(F32)
    low = jnp.concatenate([low[:, :rank], low[:, rank:]], axis=0)
    chosen = marks[...].astype(F32)
    base = own[...]
    for j in range(pairs):
        both = jnp.concatenate([refs[2 * j][...], refs[2 * j + 1][...]], axis=0)
        base = base + both.astype(F32)
    first = 0
    for up in ups:
        held = up.shape[0] // rank
        spread = jnp.concatenate(
            [low * chosen[:, y : y + 1] for y in range(first, first + held)], axis=1
        ).astype(BF16)
        base = base + contract(spread, up[...], 1, 0)
        first += held
    out[...] = base.reshape(out.shape).astype(BF16)


def combine(marks, own, halves, lows, ups, steps):
    rows, columns = own.shape
    split = [part for pair in halves for part in pair]
    inputs = [marks, own, *split, *lows, *ups]
    return pl.pallas_call(
        functools.partial(combine_kernel, len(halves), len(lows)),
        out_shape=jax.ShapeDtypeStruct((rows // steps, steps, columns), BF16),
        compiler_params=pltpu.CompilerParams(vmem_limit_bytes=SMALL_VMEM),
        cost_estimate=SMALL_COST,
        name="combine",
    )(*inputs)


def swap(value, axis, k):
    count = lax.axis_size(axis)
    return lax.ppermute(value, axis, [(i, i ^ k) for i in range(count)])


def forward(held, axis, bit):
    while bit:
        for k in list(held):
            if k ^ bit not in held:
                held[k ^ bit] = swap(held[k], axis, bit)
        bit //= 2


def body(
    queries,
    token_key_rows,
    token_value_rows,
    cached_key_rows,
    cached_value_rows,
    cache_length,
    request_adapter,
    output_weight_matrix,
    adapter_down_weight,
    adapter_up_weight,
):
    requests, steps, _ = queries.shape
    owners = lax.axis_size("adapter")
    blocks = lax.axis_size("tensor")
    resident, rank, columns = adapter_up_weight.shape
    place = lax.axis_index("adapter").reshape(1)
    mine = lax.axis_index("tensor").reshape(1)

    top_bit = owners // 2
    ups = {0: adapter_up_weight.reshape(resident * rank, columns)}
    downs = {0: adapter_down_weight.reshape(resident * rank, -1)}
    downs[top_bit] = swap(downs[0], "adapter", top_bit)
    cut = resident * rank // 2
    far_ups = [{top_bit: swap(ups[0][:cut], "adapter", top_bit)}]
    for held in (downs, ups):
        held[1] = swap(held[0], "adapter", 1)

    attended, marks, first = attend(
        queries,
        token_key_rows,
        token_value_rows,
        cached_key_rows,
        cached_value_rows,
        output_weight_matrix,
        cache_length,
        place,
        mine,
        request_adapter,
        resident,
        blocks,
        columns,
    )
    ups[1], downs[1], attended, first = lax.optimization_barrier(
        (ups[1], downs[1], attended, first)
    )
    inward = {blocks - 1: swap(first, "tensor", 1)}
    made = project(attended, output_weight_matrix, mine, blocks)
    partials = {blocks - 2 - j: part for j, part in enumerate(made)}
    for k in range(blocks - 3, 1, -2):
        inward[k] = swap(partials[k], "tensor", 1)
    partials, inward = lax.optimization_barrier((partials, inward))
    half = requests * steps // 2
    top, bottom = [], []
    for k in range(2, blocks, 2):
        pair = partials[k].astype(F32) + inward[k + 1].astype(F32)
        pair = pair.astype(BF16)
        top.append(swap(pair[:half], "tensor", k))
        bottom.append(swap(pair[half:], "tensor", k))
    near = swap(partials[1], "tensor", 1)
    near = near.astype(F32) + partials[0].astype(F32)
    last_ups, far_ups[0] = lax.optimization_barrier((ups[0][cut:], far_ups[0]))
    far_ups.append({top_bit: swap(last_ups, "adapter", top_bit)})
    downs[top_bit], far_ups[0], top = lax.optimization_barrier(
        (downs[top_bit], far_ups[0], top)
    )
    forward(downs, "adapter", top_bit // 2)
    forward(far_ups[0], "adapter", top_bit // 2)
    low = low_partial(attended, marks, [downs[k] for k in range(owners)], rank)
    low, bottom, far_ups = lax.optimization_barrier((low, bottom, far_ups))
    low_parts = [low] + [swap(low, "tensor", k) for k in range(1, blocks)]
    forward(ups, "adapter", top_bit // 2)
    for held in far_ups:
        forward(held, "adapter", top_bit // 2)
    pieces = []
    for k in range(owners):
        pieces += [ups[k]] if k < top_bit else [held[k] for held in far_ups]
    return combine(marks, near, [*zip(top, bottom)], low_parts, pieces, steps)


def solution(mesh):
    rows = P(("group", "adapter"), None, "tensor")
    return jax.shard_map(
        body,
        mesh=mesh,
        in_specs=(
            rows,
            rows,
            rows,
            rows,
            rows,
            P(("group", "adapter")),
            P(("group", "adapter")),
            P("tensor", None),
            rows,
            rows,
        ),
        out_specs=rows,
        check_vma=False,
    )
```

```python
import functools
import math

import jax
import jax.numpy as jnp
from jax import lax
from jax.experimental import pallas as pl
from jax.experimental.pallas import tpu as pltpu
from jax.sharding import PartitionSpec as P

HEAD_DIM = 128
AHEAD = 4
NEGATIVE = -1e30
LANES = 128
KERNEL_VMEM = 56 * 1024 * 1024
SMALL_COST = pl.CostEstimate(flops=1024, bytes_accessed=1024, transcendentals=0)
SMALL_VMEM = 16 * 1024 * 1024

F32 = jnp.float32
BF16 = jnp.bfloat16


def contract(a, b, a_dim, b_dim):
    return lax.dot_general(
        a, b, (((a_dim,), (b_dim,)), ((), ())), preferred_element_type=F32
    )


def attend_kernel(
    made,
    resident,
    block,
    lengths,
    place,
    column,
    adapters,
    queries_hbm,
    fresh_k_hbm,
    fresh_v_hbm,
    cache_k_hbm,
    cache_v_hbm,
    weight_hbm,
    *rest,
):
    attended, marks_out, partial = rest[:3]
    (
        queries,
        fresh_k,
        fresh_v,
        cache_k,
        cache_v,
        weight,
        new_k,
        new_v,
        query_scratch,
        result_scratch,
        small_sem,
        cache_sem,
        weight_sem,
    ) = rest[3:]
    requests, steps, width = queries.shape
    heads = width // HEAD_DIM
    groups = cache_k.shape[2] // HEAD_DIM
    sharing = heads // groups
    cache_size = cache_k.shape[1]
    rows = block * steps
    total_rows = requests * steps
    span = steps * sharing
    chunks = requests // block
    columns = weight.shape[1]

    def cache_copies(i):
        part = pl.ds(i * block, block)
        return (
            pltpu.make_async_copy(cache_k_hbm.at[part], cache_k.at[part], cache_sem.at[0, i]),
            pltpu.make_async_copy(cache_v_hbm.at[part], cache_v.at[part], cache_sem.at[1, i]),
        )

    small = [
        pltpu.make_async_copy(queries_hbm, queries, small_sem.at[0]),
        pltpu.make_async_copy(fresh_k_hbm, fresh_k, small_sem.at[1]),
        pltpu.make_async_copy(fresh_v_hbm, fresh_v, small_sem.at[2]),
    ]
    start = pl.multiple_of(jnp.bitwise_xor(column[0], made) * columns, LANES)
    weight_copy = pltpu.make_async_copy(
        weight_hbm.at[:, pl.ds(start, columns)], weight, weight_sem.at[0]
    )
    for copy in (*small, *cache_copies(0)):
        copy.start()

    named = adapters[...]
    owner = lax.div(named, resident)
    local = named - owner * resident
    relative = jnp.bitwise_xor(owner, place[0]) * resident + local
    facts = jnp.concatenate(
        [relative.astype(F32), jnp.zeros((7, requests), F32)], axis=0
    ).astype(BF16)
    spread = lax.broadcasted_iota(jnp.int32, (requests, total_rows), 0) == lax.div(
        lax.broadcasted_iota(jnp.int32, (requests, total_rows), 1), steps
    )
    facts = contract(facts, spread.astype(BF16), 1, 0).astype(jnp.int32)
    named_here = (
        lax.broadcasted_iota(jnp.int32, (LANES, total_rows), 0) == facts[0:1]
    ).astype(BF16)
    identity = lax.broadcasted_iota(jnp.int32, (total_rows, total_rows), 0) == (
        lax.broadcasted_iota(jnp.int32, (total_rows, total_rows), 1)
    )
    marks_out[...] = contract(identity.astype(BF16), named_here, 1, 1).astype(BF16)

    positions = lax.broadcasted_iota(jnp.int32, (groups * span, cache_size), 1)
    row_id = lax.broadcasted_iota(jnp.int32, (block * groups * span, total_rows), 0)
    col_id = lax.broadcasted_iota(jnp.int32, (block * groups * span, total_rows), 1)
    distance = lax.div(row_id, groups * span) - lax.div(col_id, steps)
    causal = lax.rem(col_id, steps) <= lax.div(lax.rem(row_id, span), sharing)
    distance = jnp.where(causal, distance, requests)
    scaling = math.log2(math.e) / math.sqrt(HEAD_DIM)
    for copy in small:
        copy.wait()
    for i in range(1, min(AHEAD, chunks)):
        for copy in cache_copies(i):
            copy.start()
    new_k[...] = fresh_k[...].reshape(total_rows, groups * HEAD_DIM)
    new_v[...] = fresh_v[...].reshape(total_rows, groups * HEAD_DIM)

    @pl.loop(0, chunks)
    def _(i):
        base = i * block
        flat = queries[pl.ds(base, block)].astype(F32).reshape(rows, width)
        for h in range(heads):
            query_scratch[h * rows : (h + 1) * rows, :] = flat[
                :, h * HEAD_DIM : (h + 1) * HEAD_DIM
            ]
        for copy in cache_copies(i):
            copy.wait()

        @pl.when(i + AHEAD < chunks)
        def _():
            for copy in cache_copies(i + AHEAD):
                copy.start()

        @pl.when(i == min(1, chunks - 1))
        def _():
            weight_copy.start()

        live_fresh = distance == -base
        empty = jnp.zeros((span, HEAD_DIM), BF16)
        wide = []
        for r in range(block):
            for g in range(groups):
                parts = []
                for s in range(steps):
                    start = g * sharing * rows + r * steps + s
                    parts.append(query_scratch[pl.ds(start, sharing, stride=rows), :])
                q = jnp.concatenate(parts, axis=0).astype(BF16)
                wide.append(
                    jnp.concatenate([q if o == g else empty for o in range(groups)], axis=1)
                )
        q = jnp.concatenate(wide, axis=0)
        fresh = jnp.where(live_fresh, contract(q, new_k[...], 1, 1), NEGATIVE)
        band = groups * span
        cached = []
        for r in range(block):
            score = contract(q[r * band : (r + 1) * band], cache_k[base + r], 1, 1)
            cached.append(jnp.where(positions < lengths[base + r], score, NEGATIVE))
        cached = jnp.concatenate(cached, axis=0)
        top = jnp.max(jnp.maximum(cached, fresh), axis=1, keepdims=True)
        cached = jnp.exp2((cached - top) * scaling)
        fresh = jnp.exp2((fresh - top) * scaling)
        scale = 1.0 / jnp.sum(cached + fresh, axis=1, keepdims=True)
        cached = cached.astype(BF16)
        out = contract(fresh.astype(BF16), new_v[...], 1, 0)
        for r in range(block):
            rows_r = slice(r * band, (r + 1) * band)
            both = (
                contract(cached[rows_r], cache_v[base + r], 1, 0) + out[rows_r]
            )
            for g in range(groups):
                for s in range(steps):
                    first = g * span + s * sharing
                    piece = both[
                        first : first + sharing, g * HEAD_DIM : (g + 1) * HEAD_DIM
                    ] * scale[r * band + first : r * band + first + sharing]
                    start = g * sharing * total_rows + (base + r) * steps + s
                    result_scratch[pl.ds(start, sharing, stride=total_rows), :] = piece

    for h in range(heads):
        attended[:, h * HEAD_DIM : (h + 1) * HEAD_DIM] = result_scratch[
            h * total_rows : (h + 1) * total_rows, :
        ].astype(BF16)
    weight_copy.wait()
    tile = min(256, columns)
    for c in range(0, columns, tile):
        partial[:, c : c + tile] = contract(
            attended[...], weight[:, c : c + tile], 1, 0
        ).astype(BF16)


def attend(
    queries,
    fresh_k,
    fresh_v,
    cache_k,
    cache_v,
    weight,
    lengths,
    place,
    column,
    adapters,
    resident,
    blocks,
    columns,
):
    requests, steps, width = queries.shape
    cache_size, kv_width = cache_k.shape[1:]
    block = min(16, requests)
    heads = width // HEAD_DIM
    total_rows = requests * steps
    anywhere = pl.BlockSpec(memory_space=pl.ANY)
    local = pl.BlockSpec(memory_space=pltpu.VMEM)
    return pl.pallas_call(
        functools.partial(attend_kernel, blocks - 1, resident, block),
        grid_spec=pltpu.PrefetchScalarGridSpec(
            num_scalar_prefetch=3,
            in_specs=[local] + [anywhere] * 6,
            out_specs=[local] * 3,
            scratch_shapes=[
                pltpu.VMEM((requests, steps, width), BF16),
                pltpu.VMEM((requests, steps, kv_width), BF16),
                pltpu.VMEM((requests, steps, kv_width), BF16),
                pltpu.VMEM((requests, cache_size, kv_width), BF16),
                pltpu.VMEM((requests, cache_size, kv_width), BF16),
                pltpu.VMEM((width, columns), BF16),
                pltpu.VMEM((total_rows, kv_width), BF16),
                pltpu.VMEM((total_rows, kv_width), BF16),
                pltpu.VMEM((heads * block * steps, HEAD_DIM), F32),
                pltpu.VMEM((heads * total_rows, HEAD_DIM), F32),
                pltpu.SemaphoreType.DMA((3,)),
                pltpu.SemaphoreType.DMA((2, requests // block)),
                pltpu.SemaphoreType.DMA((1,)),
            ],
        ),
        out_shape=[
            jax.ShapeDtypeStruct((total_rows, width), BF16),
            jax.ShapeDtypeStruct((total_rows, LANES), BF16),
            jax.ShapeDtypeStruct((total_rows, columns), BF16),
        ],
        compiler_params=pltpu.CompilerParams(vmem_limit_bytes=KERNEL_VMEM),
        cost_estimate=SMALL_COST,
        name="attend",
    )(
        lengths,
        place,
        column,
        adapters.reshape(1, requests),
        queries,
        fresh_k,
        fresh_v,
        cache_k,
        cache_v,
        weight,
    )


def project_kernel(count, *refs):
    column = refs[0]
    refs = refs[1:]
    attended_hbm, weight_hbm = refs[:2]
    outs = refs[2 : 2 + count]
    attended, weight, in_sem, weight_sem = refs[2 + count :]
    columns = weight.shape[2]
    attended_copy = pltpu.make_async_copy(attended_hbm, attended, in_sem.at[0])
    attended_copy.start()
    copies = []
    for j in range(count):
        start = pl.multiple_of(jnp.bitwise_xor(column[0], count - 1 - j) * columns, LANES)
        copy = pltpu.make_async_copy(
            weight_hbm.at[:, pl.ds(start, columns)], weight.at[j], weight_sem.at[j]
        )
        copy.start()
        copies.append(copy)
    attended_copy.wait()
    tile = min(256, columns)
    for j in range(count):
        copies[j].wait()
        for c in range(0, columns, tile):
            outs[j][:, c : c + tile] = contract(
                attended[...], weight[j, :, c : c + tile], 1, 0
            ).astype(BF16)


def project(attended, weight, column, blocks):
    rows, depth = attended.shape
    columns = weight.shape[1] // blocks
    count = blocks - 1
    local = pl.BlockSpec(memory_space=pltpu.VMEM)
    anywhere = pl.BlockSpec(memory_space=pl.ANY)
    return pl.pallas_call(
        functools.partial(project_kernel, count),
        grid_spec=pltpu.PrefetchScalarGridSpec(
            num_scalar_prefetch=1,
            in_specs=[anywhere] * 2,
            out_specs=[local] * count,
            scratch_shapes=[
                pltpu.VMEM((rows, depth), BF16),
                pltpu.VMEM((count, depth, columns), BF16),
                pltpu.SemaphoreType.DMA((1,)),
                pltpu.SemaphoreType.DMA((count,)),
            ],
        ),
        out_shape=[jax.ShapeDtypeStruct((rows, columns), BF16)] * count,
        compiler_params=pltpu.CompilerParams(vmem_limit_bytes=KERNEL_VMEM),
        cost_estimate=SMALL_COST,
        name="project",
    )(column, attended, weight)


def low_kernel(rank, attended, marks, *refs):
    out = refs[-1]
    rows = attended[...]
    chosen = marks[...].astype(F32)
    low = jnp.zeros((rows.shape[0], rank), F32)
    first = 0
    for down in refs[:-1]:
        every = contract(rows, down[...], 1, 1)
        for y in range(down.shape[0] // rank):
            part = every[:, y * rank : (y + 1) * rank]
            low = low + part * chosen[:, first : first + 1]
            first += 1
    half = low.shape[0] // 2
    out[...] = jnp.concatenate([low[:half], low[half:]], axis=1).astype(BF16)


def low_partial(attended, marks, downs, rank):
    rows = attended.shape[0]
    return pl.pallas_call(
        functools.partial(low_kernel, rank),
        out_shape=jax.ShapeDtypeStruct((rows // 2, 2 * rank), BF16),
        compiler_params=pltpu.CompilerParams(vmem_limit_bytes=SMALL_VMEM),
        cost_estimate=SMALL_COST,
        name="low",
    )(attended, marks, *downs)


def combine_kernel(sums, blocks, marks, *refs):
    partials = refs[:sums]
    lows = refs[sums : sums + blocks]
    ups = refs[sums + blocks : -1]
    out = refs[-1]
    low = lows[0][...].astype(F32)
    for part in lows[1:]:
        low = low + part[...].astype(F32)
    rank = low.shape[1] // 2
    low = low.astype(BF16).astype(F32)
    low = jnp.concatenate([low[:, :rank], low[:, rank:]], axis=0)
    chosen = marks[...].astype(F32)
    base = partials[0][...].astype(F32)
    for part in partials[1:]:
        base = base + part[...].astype(F32)
    first = 0
    for up in ups:
        held = up.shape[0] // rank
        spread = jnp.concatenate(
            [low * chosen[:, y : y + 1] for y in range(first, first + held)], axis=1
        ).astype(BF16)
        base = base + contract(spread, up[...], 1, 0)
        first += held
    out[...] = base.reshape(out.shape).astype(BF16)


def combine(marks, own, partials, lows, ups, steps):
    rows, columns = own.shape
    inputs = [marks, own, *partials, *lows, *ups]
    return pl.pallas_call(
        functools.partial(combine_kernel, 1 + len(partials), len(lows)),
        out_shape=jax.ShapeDtypeStruct((rows // steps, steps, columns), BF16),
        compiler_params=pltpu.CompilerParams(vmem_limit_bytes=SMALL_VMEM),
        cost_estimate=SMALL_COST,
        name="combine",
    )(*inputs)


def swap(value, axis, k):
    count = lax.axis_size(axis)
    return lax.ppermute(value, axis, [(i, i ^ k) for i in range(count)])


def forward(held, axis, bit):
    while bit:
        for k in list(held):
            if k ^ bit not in held:
                held[k ^ bit] = swap(held[k], axis, bit)
        bit //= 2


def body(
    queries,
    token_key_rows,
    token_value_rows,
    cached_key_rows,
    cached_value_rows,
    cache_length,
    request_adapter,
    output_weight_matrix,
    adapter_down_weight,
    adapter_up_weight,
):
    requests, steps, _ = queries.shape
    owners = lax.axis_size("adapter")
    blocks = lax.axis_size("tensor")
    resident, rank, columns = adapter_up_weight.shape
    place = lax.axis_index("adapter").reshape(1)
    mine = lax.axis_index("tensor").reshape(1)

    top_bit = owners // 2
    ups = {0: adapter_up_weight.reshape(resident * rank, columns)}
    downs = {0: adapter_down_weight.reshape(resident * rank, -1)}
    downs[top_bit] = swap(downs[0], "adapter", top_bit)
    cut = (resident - 1) * rank
    far_ups = [{top_bit: swap(ups[0][:cut], "adapter", top_bit)}]
    for held in (downs, ups):
        held[1] = swap(held[0], "adapter", 1)

    attended, marks, first = attend(
        queries,
        token_key_rows,
        token_value_rows,
        cached_key_rows,
        cached_value_rows,
        output_weight_matrix,
        cache_length,
        place,
        mine,
        request_adapter,
        resident,
        blocks,
        columns,
    )
    ups[1], downs[1], attended, first = lax.optimization_barrier(
        (ups[1], downs[1], attended, first)
    )
    inward = {blocks - 1: swap(first, "tensor", 1)}
    made = project(attended, output_weight_matrix, mine, blocks)
    partials = {blocks - 2 - j: part for j, part in enumerate(made)}
    for k in range(blocks - 3, 1, -2):
        inward[k] = swap(partials[k], "tensor", 1)
    partials, inward = lax.optimization_barrier((partials, inward))
    outward = []
    for k in range(2, blocks, 2):
        pair = partials[k].astype(F32) + inward[k + 1].astype(F32)
        outward.append(swap(pair.astype(BF16), "tensor", k))
    near = swap(partials[1], "tensor", 1)
    near = near.astype(F32) + partials[0].astype(F32)
    downs[top_bit], far_ups[0], inw = lax.optimization_barrier((downs[top_bit], far_ups[0], outward))
    outward = inw
    forward(downs, "adapter", top_bit // 2)
    last_ups, outward = lax.optimization_barrier((ups[0][cut:], outward))
    far_ups.append({top_bit: swap(last_ups, "adapter", top_bit)})
    low = low_partial(attended, marks, [downs[k] for k in range(owners)], rank)
    far_ups, low = lax.optimization_barrier((far_ups, low))
    low_parts = [low] + [swap(low, "tensor", k) for k in range(1, blocks)]
    forward(ups, "adapter", top_bit // 2)
    for held in far_ups:
        forward(held, "adapter", top_bit // 2)
    pieces = []
    for k in range(owners):
        pieces += [ups[k]] if k < top_bit else [held[k] for held in far_ups]
    return combine(marks, near, outward, low_parts, pieces, steps)


def solution(mesh):
    rows = P(("group", "adapter"), None, "tensor")
    return jax.shard_map(
        body,
        mesh=mesh,
        in_specs=(
            rows,
            rows,
            rows,
            rows,
            rows,
            P(("group", "adapter")),
            P(("group", "adapter")),
            P("tensor", None),
            rows,
            rows,
        ),
        out_specs=rows,
        check_vma=False,
    )
```

```python
import functools
import math

import jax
import jax.numpy as jnp
from jax import lax
from jax.experimental import pallas as pl
from jax.experimental.pallas import tpu as pltpu
from jax.sharding import PartitionSpec as P

HEAD_DIM = 128
AHEAD = 4
NEGATIVE = -1e30
LANES = 128
KERNEL_VMEM = 56 * 1024 * 1024
PROJECT_VMEM = 50 * 1024 * 1024
SMALL_COST = pl.CostEstimate(flops=1024, bytes_accessed=1024, transcendentals=0)
SMALL_VMEM = 16 * 1024 * 1024

F32 = jnp.float32
BF16 = jnp.bfloat16


def contract(a, b, a_dim, b_dim):
    return lax.dot_general(
        a, b, (((a_dim,), (b_dim,)), ((), ())), preferred_element_type=F32
    )


def attend_kernel(
    made,
    resident,
    block,
    lengths,
    place,
    column,
    adapters,
    queries_hbm,
    fresh_k_hbm,
    fresh_v_hbm,
    cache_k_hbm,
    cache_v_hbm,
    weight_hbm,
    *rest,
):
    attended, marks_out, partial = rest[:3]
    (
        queries,
        fresh_k,
        fresh_v,
        cache_k,
        cache_v,
        weight,
        new_k,
        new_v,
        query_scratch,
        result_scratch,
        small_sem,
        cache_sem,
        weight_sem,
    ) = rest[3:]
    requests, steps, width = queries.shape
    heads = width // HEAD_DIM
    groups = cache_k.shape[2] // HEAD_DIM
    sharing = heads // groups
    cache_size = cache_k.shape[1]
    rows = block * steps
    total_rows = requests * steps
    span = steps * sharing
    chunks = requests // block
    columns = weight.shape[1]

    def cache_copies(i):
        part = pl.ds(i * block, block)
        return (
            pltpu.make_async_copy(cache_k_hbm.at[part], cache_k.at[part], cache_sem.at[0, i]),
            pltpu.make_async_copy(cache_v_hbm.at[part], cache_v.at[part], cache_sem.at[1, i]),
        )

    small = [
        pltpu.make_async_copy(queries_hbm, queries, small_sem.at[0]),
        pltpu.make_async_copy(fresh_k_hbm, fresh_k, small_sem.at[1]),
        pltpu.make_async_copy(fresh_v_hbm, fresh_v, small_sem.at[2]),
    ]
    start = pl.multiple_of(jnp.bitwise_xor(column[0], made) * columns, LANES)
    weight_copy = pltpu.make_async_copy(
        weight_hbm.at[:, pl.ds(start, columns)], weight, weight_sem.at[0]
    )
    for copy in (*small, *cache_copies(0)):
        copy.start()

    named = adapters[...]
    owner = lax.div(named, resident)
    local = named - owner * resident
    relative = jnp.bitwise_xor(owner, place[0]) * resident + local
    facts = jnp.concatenate(
        [relative.astype(F32), jnp.zeros((7, requests), F32)], axis=0
    ).astype(BF16)
    spread = lax.broadcasted_iota(jnp.int32, (requests, total_rows), 0) == lax.div(
        lax.broadcasted_iota(jnp.int32, (requests, total_rows), 1), steps
    )
    facts = contract(facts, spread.astype(BF16), 1, 0).astype(jnp.int32)
    named_here = (
        lax.broadcasted_iota(jnp.int32, (LANES, total_rows), 0) == facts[0:1]
    ).astype(BF16)
    identity = lax.broadcasted_iota(jnp.int32, (total_rows, total_rows), 0) == (
        lax.broadcasted_iota(jnp.int32, (total_rows, total_rows), 1)
    )
    marks_out[...] = contract(identity.astype(BF16), named_here, 1, 1).astype(BF16)

    positions = lax.broadcasted_iota(jnp.int32, (groups * span, cache_size), 1)
    row_id = lax.broadcasted_iota(jnp.int32, (block * groups * span, total_rows), 0)
    col_id = lax.broadcasted_iota(jnp.int32, (block * groups * span, total_rows), 1)
    distance = lax.div(row_id, groups * span) - lax.div(col_id, steps)
    causal = lax.rem(col_id, steps) <= lax.div(lax.rem(row_id, span), sharing)
    distance = jnp.where(causal, distance, requests)
    scaling = math.log2(math.e) / math.sqrt(HEAD_DIM)
    for copy in small:
        copy.wait()
    for i in range(1, min(AHEAD, chunks)):
        for copy in cache_copies(i):
            copy.start()
    new_k[...] = fresh_k[...].reshape(total_rows, groups * HEAD_DIM)
    new_v[...] = fresh_v[...].reshape(total_rows, groups * HEAD_DIM)

    @pl.loop(0, chunks)
    def _(i):
        base = i * block
        flat = queries[pl.ds(base, block)].astype(F32).reshape(rows, width)
        for h in range(heads):
            query_scratch[h * rows : (h + 1) * rows, :] = flat[
                :, h * HEAD_DIM : (h + 1) * HEAD_DIM
            ]
        for copy in cache_copies(i):
            copy.wait()

        @pl.when(i + AHEAD < chunks)
        def _():
            for copy in cache_copies(i + AHEAD):
                copy.start()

        @pl.when(i == min(1, chunks - 1))
        def _():
            weight_copy.start()

        live_fresh = distance == -base
        empty = jnp.zeros((span, HEAD_DIM), BF16)
        wide = []
        for r in range(block):
            for g in range(groups):
                parts = []
                for s in range(steps):
                    start = g * sharing * rows + r * steps + s
                    parts.append(query_scratch[pl.ds(start, sharing, stride=rows), :])
                q = jnp.concatenate(parts, axis=0).astype(BF16)
                wide.append(
                    jnp.concatenate([q if o == g else empty for o in range(groups)], axis=1)
                )
        q = jnp.concatenate(wide, axis=0)
        fresh = jnp.where(live_fresh, contract(q, new_k[...], 1, 1), NEGATIVE)
        band = groups * span
        cached = []
        for r in range(block):
            score = contract(q[r * band : (r + 1) * band], cache_k[base + r], 1, 1)
            cached.append(jnp.where(positions < lengths[base + r], score, NEGATIVE))
        cached = jnp.concatenate(cached, axis=0)
        top = jnp.max(jnp.maximum(cached, fresh), axis=1, keepdims=True)
        cached = jnp.exp2((cached - top) * scaling)
        fresh = jnp.exp2((fresh - top) * scaling)
        scale = 1.0 / jnp.sum(cached + fresh, axis=1, keepdims=True)
        cached = cached.astype(BF16)
        out = contract(fresh.astype(BF16), new_v[...], 1, 0)
        for r in range(block):
            rows_r = slice(r * band, (r + 1) * band)
            both = (
                contract(cached[rows_r], cache_v[base + r], 1, 0) + out[rows_r]
            )
            for g in range(groups):
                for s in range(steps):
                    first = g * span + s * sharing
                    piece = both[
                        first : first + sharing, g * HEAD_DIM : (g + 1) * HEAD_DIM
                    ] * scale[r * band + first : r * band + first + sharing]
                    start = g * sharing * total_rows + (base + r) * steps + s
                    result_scratch[pl.ds(start, sharing, stride=total_rows), :] = piece

    for h in range(heads):
        attended[:, h * HEAD_DIM : (h + 1) * HEAD_DIM] = result_scratch[
            h * total_rows : (h + 1) * total_rows, :
        ].astype(BF16)
    weight_copy.wait()
    tile = min(256, columns)
    for c in range(0, columns, tile):
        partial[:, c : c + tile] = contract(
            attended[...], weight[:, c : c + tile], 1, 0
        ).astype(BF16)


def attend(
    queries,
    fresh_k,
    fresh_v,
    cache_k,
    cache_v,
    weight,
    lengths,
    place,
    column,
    adapters,
    resident,
    blocks,
    columns,
):
    requests, steps, width = queries.shape
    cache_size, kv_width = cache_k.shape[1:]
    block = min(16, requests)
    heads = width // HEAD_DIM
    total_rows = requests * steps
    anywhere = pl.BlockSpec(memory_space=pl.ANY)
    local = pl.BlockSpec(memory_space=pltpu.VMEM)
    return pl.pallas_call(
        functools.partial(attend_kernel, blocks - 1, resident, block),
        grid_spec=pltpu.PrefetchScalarGridSpec(
            num_scalar_prefetch=3,
            in_specs=[local] + [anywhere] * 6,
            out_specs=[local] * 3,
            scratch_shapes=[
                pltpu.VMEM((requests, steps, width), BF16),
                pltpu.VMEM((requests, steps, kv_width), BF16),
                pltpu.VMEM((requests, steps, kv_width), BF16),
                pltpu.VMEM((requests, cache_size, kv_width), BF16),
                pltpu.VMEM((requests, cache_size, kv_width), BF16),
                pltpu.VMEM((width, columns), BF16),
                pltpu.VMEM((total_rows, kv_width), BF16),
                pltpu.VMEM((total_rows, kv_width), BF16),
                pltpu.VMEM((heads * block * steps, HEAD_DIM), F32),
                pltpu.VMEM((heads * total_rows, HEAD_DIM), F32),
                pltpu.SemaphoreType.DMA((3,)),
                pltpu.SemaphoreType.DMA((2, requests // block)),
                pltpu.SemaphoreType.DMA((1,)),
            ],
        ),
        out_shape=[
            jax.ShapeDtypeStruct((total_rows, width), BF16),
            jax.ShapeDtypeStruct((total_rows, LANES), BF16),
            jax.ShapeDtypeStruct((total_rows, columns), BF16),
        ],
        compiler_params=pltpu.CompilerParams(vmem_limit_bytes=KERNEL_VMEM),
        cost_estimate=SMALL_COST,
        name="attend",
    )(
        lengths,
        place,
        column,
        adapters.reshape(1, requests),
        queries,
        fresh_k,
        fresh_v,
        cache_k,
        cache_v,
        weight,
    )


def project_kernel(count, *refs):
    column = refs[0]
    refs = refs[1:]
    attended_hbm, weight_hbm = refs[:2]
    outs = refs[2 : 2 + count]
    attended, weight, in_sem, weight_sem = refs[2 + count :]
    columns = weight.shape[2]
    attended_copy = pltpu.make_async_copy(attended_hbm, attended, in_sem.at[0])
    attended_copy.start()
    copies = []
    for j in range(count):
        start = pl.multiple_of(jnp.bitwise_xor(column[0], count - 1 - j) * columns, LANES)
        copy = pltpu.make_async_copy(
            weight_hbm.at[:, pl.ds(start, columns)], weight.at[j], weight_sem.at[j]
        )
        copy.start()
        copies.append(copy)
    attended_copy.wait()
    tile = min(256, columns)
    for j in range(count):
        copies[j].wait()
        for c in range(0, columns, tile):
            outs[j][:, c : c + tile] = contract(
                attended[...], weight[j, :, c : c + tile], 1, 0
            ).astype(BF16)


def project(attended, weight, column, blocks):
    rows, depth = attended.shape
    columns = weight.shape[1] // blocks
    count = blocks - 1
    local = pl.BlockSpec(memory_space=pltpu.VMEM)
    anywhere = pl.BlockSpec(memory_space=pl.ANY)
    return pl.pallas_call(
        functools.partial(project_kernel, count),
        grid_spec=pltpu.PrefetchScalarGridSpec(
            num_scalar_prefetch=1,
            in_specs=[anywhere] * 2,
            out_specs=[local] * count,
            scratch_shapes=[
                pltpu.VMEM((rows, depth), BF16),
                pltpu.VMEM((count, depth, columns), BF16),
                pltpu.SemaphoreType.DMA((1,)),
                pltpu.SemaphoreType.DMA((count,)),
            ],
        ),
        out_shape=[jax.ShapeDtypeStruct((rows, columns), BF16)] * count,
        compiler_params=pltpu.CompilerParams(vmem_limit_bytes=PROJECT_VMEM),
        cost_estimate=SMALL_COST,
        name="project",
    )(column, attended, weight)


def low_kernel(rank, attended, marks, *refs):
    out = refs[-1]
    rows = attended[...]
    chosen = marks[...].astype(F32)
    low = jnp.zeros((rows.shape[0], rank), F32)
    first = 0
    for down in refs[:-1]:
        every = contract(rows, down[...], 1, 1)
        for y in range(down.shape[0] // rank):
            part = every[:, y * rank : (y + 1) * rank]
            low = low + part * chosen[:, first : first + 1]
            first += 1
    half = low.shape[0] // 2
    out[...] = jnp.concatenate([low[:half], low[half:]], axis=1).astype(BF16)


def low_partial(attended, marks, downs, rank):
    rows = attended.shape[0]
    return pl.pallas_call(
        functools.partial(low_kernel, rank),
        out_shape=jax.ShapeDtypeStruct((rows // 2, 2 * rank), BF16),
        compiler_params=pltpu.CompilerParams(vmem_limit_bytes=SMALL_VMEM),
        cost_estimate=SMALL_COST,
        name="low",
    )(attended, marks, *downs)


def combine_kernel(sums, blocks, marks, *refs):
    partials = refs[:sums]
    lows = refs[sums : sums + blocks]
    ups = refs[sums + blocks : -1]
    out = refs[-1]
    low = lows[0][...].astype(F32)
    for part in lows[1:]:
        low = low + part[...].astype(F32)
    rank = low.shape[1] // 2
    low = low.astype(BF16).astype(F32)
    low = jnp.concatenate([low[:, :rank], low[:, rank:]], axis=0)
    chosen = marks[...].astype(F32)
    base = partials[0][...].astype(F32)
    for part in partials[1:]:
        base = base + part[...].astype(F32)
    first = 0
    for up in ups:
        held = up.shape[0] // rank
        spread = jnp.concatenate(
            [low * chosen[:, y : y + 1] for y in range(first, first + held)], axis=1
        ).astype(BF16)
        base = base + contract(spread, up[...], 1, 0)
        first += held
    out[...] = base.reshape(out.shape).astype(BF16)


def combine(marks, own, partials, lows, ups, steps):
    rows, columns = own.shape
    inputs = [marks, own, *partials, *lows, *ups]
    return pl.pallas_call(
        functools.partial(combine_kernel, 1 + len(partials), len(lows)),
        out_shape=jax.ShapeDtypeStruct((rows // steps, steps, columns), BF16),
        compiler_params=pltpu.CompilerParams(vmem_limit_bytes=SMALL_VMEM),
        cost_estimate=SMALL_COST,
        name="combine",
    )(*inputs)


def swap(value, axis, k):
    count = lax.axis_size(axis)
    return lax.ppermute(value, axis, [(i, i ^ k) for i in range(count)])


def forward(held, axis, bit):
    while bit:
        for k in list(held):
            if k ^ bit not in held:
                held[k ^ bit] = swap(held[k], axis, bit)
        bit //= 2


def body(
    queries,
    token_key_rows,
    token_value_rows,
    cached_key_rows,
    cached_value_rows,
    cache_length,
    request_adapter,
    output_weight_matrix,
    adapter_down_weight,
    adapter_up_weight,
):
    requests, steps, _ = queries.shape
    owners = lax.axis_size("adapter")
    blocks = lax.axis_size("tensor")
    resident, rank, columns = adapter_up_weight.shape
    place = lax.axis_index("adapter").reshape(1)
    mine = lax.axis_index("tensor").reshape(1)

    top_bit = owners // 2
    ups = {0: adapter_up_weight.reshape(resident * rank, columns)}
    downs = {0: adapter_down_weight.reshape(resident * rank, -1)}
    downs[top_bit] = swap(downs[0], "adapter", top_bit)
    cut = (resident - 1) * rank
    far_ups = [{top_bit: swap(ups[0][:cut], "adapter", top_bit)}]
    for held in (downs, ups):
        held[1] = swap(held[0], "adapter", 1)

    attended, marks, first = attend(
        queries,
        token_key_rows,
        token_value_rows,
        cached_key_rows,
        cached_value_rows,
        output_weight_matrix,
        cache_length,
        place,
        mine,
        request_adapter,
        resident,
        blocks,
        columns,
    )
    ups[1], downs[1], attended, first = lax.optimization_barrier(
        (ups[1], downs[1], attended, first)
    )
    inward = {blocks - 1: swap(first, "tensor", 1)}
    made = project(attended, output_weight_matrix, mine, blocks)
    partials = {blocks - 2 - j: part for j, part in enumerate(made)}
    for k in range(blocks - 3, 1, -2):
        inward[k] = swap(partials[k], "tensor", 1)
    partials, inward = lax.optimization_barrier((partials, inward))
    outward = []
    for k in range(2, blocks, 2):
        pair = partials[k].astype(F32) + inward[k + 1].astype(F32)
        outward.append(swap(pair.astype(BF16), "tensor", k))
    near = swap(partials[1], "tensor", 1)
    near = near.astype(F32) + partials[0].astype(F32)
    downs[top_bit], far_ups[0], inw = lax.optimization_barrier((downs[top_bit], far_ups[0], outward))
    outward = inw
    forward(downs, "adapter", top_bit // 2)
    last_ups, outward = lax.optimization_barrier((ups[0][cut:], outward))
    far_ups.append({top_bit: swap(last_ups, "adapter", top_bit)})
    low = low_partial(attended, marks, [downs[k] for k in range(owners)], rank)
    far_ups, low = lax.optimization_barrier((far_ups, low))
    low_parts = [low] + [swap(low, "tensor", k) for k in range(1, blocks)]
    forward(ups, "adapter", top_bit // 2)
    for held in far_ups:
        forward(held, "adapter", top_bit // 2)
    pieces = []
    for k in range(owners):
        pieces += [ups[k]] if k < top_bit else [held[k] for held in far_ups]
    return combine(marks, near, outward, low_parts, pieces, steps)


def solution(mesh):
    rows = P(("group", "adapter"), None, "tensor")
    return jax.shard_map(
        body,
        mesh=mesh,
        in_specs=(
            rows,
            rows,
            rows,
            rows,
            rows,
            P(("group", "adapter")),
            P(("group", "adapter")),
            P("tensor", None),
            rows,
            rows,
        ),
        out_specs=rows,
        check_vma=False,
    )
```
